512 devices in a mesh: lon: 64 (over z, y_hi, core), lat: 8 (over y_lo, x).
Axes of the slice: x: 4, y: 4 (y_hi: 2, y_lo: 2; y = y_hi * 2 + y_lo), z: 16, core: 2. Of those that a mesh axis runs over, the one named last changes fastest.
Arguments:
- patches: bfloat16 [768, 96, 2, 512], P('lon', 'lat'), may hold values from -6 to 6
- qkv_first: bfloat16 [512, 1536], P(None, 'lon'), may hold values from -2 to 2
- proj_first: bfloat16 [512, 512], P(None, 'lon'), may hold values from -1 to 1
- qkv_second: bfloat16 [512, 1536], P(None, 'lon'), may hold values from -2 to 2
- proj_second: bfloat16 [512, 512], P(None, 'lon'), may hold values from -1 to 1
- merge_weight: bfloat16 [2048, 1024], P(None, 'lon'), may hold values from -0.125 to 0.125
Outputs:
- merged: bfloat16 [384, 48, 2, 1024], P('lon', 'lat')
The draws below stay inside these ranges and needn't reach their ends.
All inputs are finite; a program needn't handle non-finite values.
Results may differ from the reference program's by a relative error of at most 0.019.
Values may be sent and summed in bfloat16 or wider, within the bound.
A program may use at most 64 MiB of HBM per device.

```python
import jax
import jax.numpy as jnp
from jax import lax

D = 512
HEADS = 16
WLON = 12
WLAT = 6
WLEV = 2
LEVELS = 2
NLON = 768
NLAT = 96


def drawn_columns(key):
    values = jax.random.normal(key, (D, 3 * D), jnp.float32) * D ** (-0.5)
    return jnp.clip(values, -1.0, 1.0)


def draw_qkv_first(key, part):
    key = jax.random.fold_in(key, 11)
    return drawn_columns(key).astype(jnp.bfloat16)


def draw_qkv_second(key, part):
    key = jax.random.fold_in(key, 23)
    return drawn_columns(key).astype(jnp.bfloat16)


def steps_of(stream_key, extent, shards, least, largest):
    gain, own = 1.0, jax.random.fold_in(stream_key, 6)
    for dim, parts in shards:
        heights = jnp.exp(jax.random.uniform(jax.random.fold_in(own, dim), (parts,), jnp.float32, least / len(shards), largest / len(shards)))
        gain = gain * jnp.repeat(heights, extent[dim] // parts).reshape([-1 if axis == dim else 1 for axis in range(len(extent))])
    return gain


def noise(rng, dims, scale, most, split=(), kind=jnp.bfloat16):
    level = steps_of(rng, dims, split, -0.22, 0.18) if split else 1.0
    entries = jax.random.normal(rng, dims, jnp.float32) * scale * level
    return jnp.minimum(jnp.maximum(entries, -most), most).astype(kind)


def setup_inputs(seed: int = 0) -> dict:
    arg_keys = jax.random.split(jax.random.key(seed), 7)
    patches = noise(arg_keys[0], (NLON, NLAT, LEVELS, D), 1.0, 6.0, ((0, 64), (1, 8)))
    qkv_first = draw_qkv_first(jax.random.fold_in(arg_keys[6], 71), 0)
    proj_first = noise(arg_keys[2], (D, D), (D // 16) ** -0.5, 1.0, ((1, 64),))
    qkv_second = draw_qkv_second(jax.random.fold_in(arg_keys[6], 71), 0)
    proj_second = noise(arg_keys[4], (D, D), (D // 16) ** -0.5, 1.0, ((1, 64),))
    merge_weight = noise(arg_keys[5], (4 * D, 2 * D), (4 * D) ** -0.5, 0.125, ((1, 64),))
    return dict(patches=patches, qkv_first=qkv_first, proj_first=proj_first, qkv_second=qkv_second, proj_second=proj_second, merge_weight=merge_weight)


norm_epsilon = 1e-05
masked_score = -1e+30

def normalize(values):
    values = values.astype(jnp.float32)
    centred = values - lax.optimization_barrier(jnp.mean(values, axis=-1, keepdims=True))
    variance = lax.optimization_barrier(jnp.mean(centred * centred, axis=-1, keepdims=True))
    return (centred * lax.rsqrt(variance + norm_epsilon)).astype(jnp.bfloat16)

def region_labels(position, count, window, offset):
    return jnp.where(position < count - window, 0, jnp.where(position < count - offset, 1, 2)).astype(jnp.int32)

def to_windows(grid):
    size_a, size_b, size_c, features = grid.shape
    grid = grid.reshape(size_a // WLON, WLON, size_b // WLAT, WLAT, size_c // WLEV, WLEV, features)
    grid = grid.transpose(0, 2, 4, 1, 3, 5, 6)
    return grid.reshape(-1, WLON * WLAT * WLEV, features)

def from_windows(flat_windows, size_a, size_b, size_c):
    features = flat_windows.shape[-1]
    grid = flat_windows.reshape(size_a // WLON, size_b // WLAT, size_c // WLEV, WLON, WLAT, WLEV, features)
    return grid.transpose(0, 3, 1, 4, 2, 5, 6).reshape(size_a, size_b, size_c, features)

def window_attend(tokens, labels, w_qkv, w_out):
    token_count = tokens.shape[0]
    width = tokens.shape[-1]
    head_size = width // HEADS
    packed = jnp.dot(normalize(tokens).astype(jnp.float32), w_qkv.astype(jnp.float32), precision=lax.Precision.HIGHEST).astype(jnp.bfloat16)
    packed = packed.astype(jnp.float32).reshape(token_count, 3, HEADS, head_size)
    scores = jnp.einsum('qhd,khd->hqk', packed[:, 0], packed[:, 1], precision=lax.Precision.HIGHEST)
    scores = scores * head_size ** (-0.5)
    same = labels[:, None] == labels[None, :]
    scores = jnp.where(same[None], scores, masked_score)
    highest = lax.optimization_barrier(jnp.max(scores, axis=-1, keepdims=True))
    weights = jnp.exp(scores - highest)
    probs = (weights / lax.optimization_barrier(jnp.sum(weights, axis=-1, keepdims=True))).astype(jnp.bfloat16)
    attended = jnp.einsum('hqk,khd->qhd', probs.astype(jnp.float32), packed[:, 2], precision=lax.Precision.HIGHEST)
    attended = attended.reshape(token_count, width).astype(jnp.bfloat16)
    update = jnp.dot(attended.astype(jnp.float32), w_out.astype(jnp.float32), precision=lax.Precision.HIGHEST)
    return (tokens.astype(jnp.float32) + update).astype(jnp.bfloat16)

def swin_block(stream, w_qkv, w_out, shifted):
    size_a, size_b, size_c, width = stream.shape
    offsets = (WLON // 2, WLAT // 2, WLEV // 2)
    if shifted:
        stream = jnp.roll(stream, (-offsets[0], -offsets[1], -offsets[2]), (0, 1, 2))
        lat_labels = region_labels(jnp.arange(size_b), size_b, WLAT, offsets[1])
        lev_labels = region_labels(jnp.arange(size_c), size_c, WLEV, offsets[2])
        labels = lat_labels[:, None] * 3 + lev_labels[None, :]
    else:
        labels = jnp.zeros((size_b, size_c), jnp.int32)
    labels = jnp.broadcast_to(labels[None, :, :, None], (size_a, size_b, size_c, 1)).astype(jnp.int32)
    window_size = WLON * WLAT * WLEV
    windows = to_windows(stream).reshape(size_a // WLON, -1, window_size, width)
    marks = to_windows(labels)[..., 0].reshape(size_a // WLON, -1, window_size)

    def column(couple):
        return jax.vmap(lambda tokens, labels_one: window_attend(tokens, labels_one, w_qkv, w_out))(couple[0], couple[1])
    result = lax.map(column, (windows, marks))
    result = from_windows(result.reshape(-1, window_size, width), size_a, size_b, size_c)
    if shifted:
        result = jnp.roll(result, offsets, (0, 1, 2))
    return result

def patch_merge(stream, w_merge):
    size_a, size_b, size_c, width = stream.shape
    blocks = stream.reshape(size_a // WLON, WLON, size_b, size_c, width)

    def one_block(block):
        quads = block.reshape(WLON // 2, 2, size_b // 2, 2, size_c, width)
        quads = quads.transpose(0, 2, 4, 3, 1, 5).reshape(-1, 4 * width)
        product = jnp.dot(normalize(quads), w_merge, preferred_element_type=jnp.float32)
        return product.astype(jnp.bfloat16).reshape(WLON // 2, size_b // 2, size_c, 2 * width)
    return lax.map(one_block, blocks).reshape(size_a // 2, size_b // 2, size_c, 2 * width)

def reference(patches, qkv_first, proj_first, qkv_second, proj_second, merge_weight):
    first = swin_block(patches, qkv_first, proj_first, False)
    second = swin_block(first, qkv_second, proj_second, True)
    return patch_merge(second, merge_weight)
```

```python
import functools

import jax
import jax.numpy as jnp
import numpy as np
from jax import lax
from jax.experimental import pallas as pl
from jax.experimental.pallas import tpu as pltpu
from jax.sharding import PartitionSpec as P

D = 512
HEADS = 16
Z = 16
H = Z // 2
Q = H // 2
L = D // 4
UNITS = 4
ROWS1 = 288
GROUP = 80
ROWS2 = 4 * GROUP
MSG = 208
EDGES = ((0, 112), (112, 48), (160, 48))
norm_epsilon = 1e-05
masked_score = -1e30
MESH = pl.DeviceIdType.MESH
F32 = jnp.float32
BF16 = jnp.bfloat16


def edge_row(lo, la, lv):
    if lo < 6 and la >= 3:
        return (lo * 9 + la - 3) * 2 + lv
    if lo >= 6 and la < 3:
        return 112 + ((lo - 6) * 3 + la) * 2 + lv
    if lo < 6:
        return 160 + (lo * 3 + la) * 2 + lv
    return None


def shifted_row(slo, q, lv):
    return ((q // 6) * 2 + lv) * GROUP + slo * 6 + q % 6


def permutations():
    send = np.zeros((MSG, ROWS1), np.float32)
    own = np.zeros((ROWS2, ROWS1), np.float32)
    arrive = np.zeros((ROWS2, MSG), np.float32)
    back = np.zeros((MSG, ROWS2), np.float32)
    quad_own = np.zeros((4 * GROUP, ROWS2), np.float32)
    quad_edge = np.zeros((4 * GROUP, MSG), np.float32)
    for lo in range(12):
        for la in range(12):
            for lv in range(2):
                first = (la // 6) * 144 + lo * 12 + (la % 6) * 2 + lv
                quad = ((la % 2) * 2 + lo % 2) * GROUP + ((lo // 2) * 6 + la // 2) * 2 + lv
                edge = edge_row(lo, la, lv)
                if edge is None:
                    second = shifted_row(lo - 6, la - 3, lv)
                    own[second, first] = 1
                    quad_own[quad, second] = 1
                else:
                    second = shifted_row((lo - 6) % 12, (la - 3) % 12, lv)
                    send[edge, first] = 1
                    arrive[second, edge] = 1
                    back[edge, second] = 1
                    quad_edge[quad, edge] = 1
    return [p.astype(jnp.bfloat16) for p in (send, own, arrive, back, quad_own, quad_edge)]


def biases():
    pad = np.zeros((GROUP, GROUP), np.float32)
    pad[:, 72:] = masked_score
    cross = np.zeros((GROUP, GROUP), np.float32)
    half = np.arange(72) % 6 < 3
    cross[:72, :72] = np.where(half[:, None] != half[None], masked_score, 0)
    return np.stack([pad, cross])


def normalize(values):
    centred = values - jnp.mean(values, axis=-1, keepdims=True)
    variance = jnp.mean(centred * centred, axis=-1, keepdims=True)
    return (centred * lax.rsqrt(variance + norm_epsilon)).astype(BF16)


def dot_nt(a, b):
    return lax.dot_general(a, b, (((1,), (1,)), ((), ())), preferred_element_type=F32)


def dot(a, b):
    return jnp.dot(a, b, preferred_element_type=F32)


def kernel(
    x_ref, a_ref, bias_ref, send_hbm, own_hbm, arrive_hbm, back_hbm, qown_hbm, qedge_hbm,
    out_ref,
    G, E, piece, qkv, mix, first, second, xn, msg_out, msg_in, ret_out, ret_in,
    p_send, p_own, p_arrive, p_back, p_qown, p_qedge,
    psem, lsem, es, er, zs, zr, p1s, p1r, p2s, p2r, p3s, p3r, ss, sr, hs, hr,
):
    lon, lat = lax.axis_index("lon"), lax.axis_index("lat")
    lons, lats = 4 * Z, 8
    c = lax.rem(lon, 2)
    yh = lax.rem(lon // 2, 2)
    z = lon // 4
    x = lax.rem(lat, 4)
    yl = lat // 4
    y = yh * 2 + yl
    lanes = pl.ds(pl.multiple_of(x * L, L), L)

    def place(x, y, z, c):
        return ((z * 2 + y // 2) * 2 + c, lax.rem(y, 2) * 4 + x)

    def wrap4(v):
        return lax.rem(v + 4, 4)

    sibling = place(x, y, z, 1 - c)
    lon_up, lon_down = lax.rem(lon + 1, lons), lax.rem(lon + lons - 1, lons)
    lat_up, lat_down = lax.rem(lat + 1, lats), lax.rem(lat + lats - 1, lats)
    halo_down = ((lon_down, lat), (lon, lat_down), (lon_down, lat_down))
    halo_up = ((lon_up, lat), (lon, lat_up), (lon_up, lat_up))

    def remote(src, dst, send, recv, device):
        return pltpu.make_async_remote_copy(
            src_ref=src, dst_ref=dst, send_sem=send, recv_sem=recv,
            device_id=device, device_id_type=MESH,
        )

    def drain(ref, sem):
        pltpu.make_async_copy(ref, ref, sem).wait()

    loads = [
        pltpu.make_async_copy(src, dst, psem.at[i])
        for i, (src, dst) in enumerate(
            (
                (send_hbm, p_send), (own_hbm, p_own), (arrive_hbm, p_arrive),
                (back_hbm, p_back), (qown_hbm, p_qown), (qedge_hbm, p_qedge),
            )
        )
    ]
    for load in loads:
        load.start()

    barrier = pltpu.get_barrier_semaphore()

    def greet(device):
        pl.semaphore_signal(barrier, inc=1, device_id=device, device_id_type=MESH)

    greet(sibling)

    @pl.loop(1, Z)
    def _(d):
        greet(place(x, y, lax.rem(z + d, Z), c))

    for d in (1, 2, 3):
        greet(place(wrap4(x + d), y, z, c))
        greet(place(x, wrap4(y + d), z, c))
    for device in halo_down + halo_up:
        greet(device)
    pl.semaphore_wait(barrier, 1 + Z - 1 + 6 + 6)

    eye = (
        lax.broadcasted_iota(jnp.int32, (128, 128), 0)
        == lax.broadcasted_iota(jnp.int32, (128, 128), 1)
    ).astype(F32).astype(BF16)
    turned = dot_nt(eye, a_ref[...])
    E[c] = turned[0:64]
    to_sibling = remote(E.at[c], E.at[c], es, er, sibling)
    to_sibling.start()

    low, high = (yl == 0).astype(F32), (yl == 1).astype(F32)
    core0, core1 = (c == 0).astype(F32), (c == 1).astype(F32)

    def put_piece(u, tile):
        tile = tile.astype(BF16)
        for k in range(4):
            piece[u, k] = tile[:, k * L : (k + 1) * L]

    for m in range(2):
        base = 64 + 32 * m
        put_piece(2 + m, turned[base : base + 16] * low + turned[base + 16 : base + 32] * high)
    to_sibling.wait()
    for s in range(2):
        r0, r1 = E[0, 32 * s : 32 * s + 32], E[1, 32 * s : 32 * s + 32]
        tile = (low * core0) * r0[0:16]
        tile += (low * core1) * jnp.concatenate([r0[16:24], r1[0:8]], axis=0)
        tile += (high * core0) * r1[8:24]
        tile += (high * core1) * jnp.concatenate([r0[24:32], r1[24:32]], axis=0)
        put_piece(s, tile)

    def zsend(u):
        slot = G.at[u, z, yh, yl, c, :, lanes]
        pltpu.make_async_copy(piece.at[u, x], slot, lsem.at[u]).start()

        @pl.loop(1, Z)
        def _(d):
            remote(
                piece.at[u, x], slot, zs.at[u], zr.at[u], place(x, y, lax.rem(z + d, Z), c)
            ).start()

    def halves(u, x, y):
        at = pl.ds(pl.multiple_of(x * L, L), L)
        return (
            G.at[u, 0:H, y // 2, lax.rem(y, 2), c, :, at],
            G.at[u, H:Z, y // 2, lax.rem(y, 2), c, :, at],
        )

    def step_a(u):
        pltpu.make_async_copy(piece.at[u, x], G.at[u, z, yh, yl, c, :, lanes], lsem.at[u]).wait()
        drain(G.at[u, 0 : Z - 1, yh, yl, c, :, lanes], zr.at[u])
        half0, half1 = halves(u, x, y)
        for d in (1, 2, 3):
            remote(half0, half0, p1s.at[u, 0], p1r.at[u, 0], place(wrap4(x + d), y, z, c)).start()
            remote(half1, half1, p1s.at[u, 1], p1r.at[u, 1], place(x, wrap4(y + d), z, c)).start()

    def wide(u, axis, at, z0, n):
        if axis == 0:
            return G.at[u, pl.ds(z0, n), at // 2, lax.rem(at, 2), c]
        span = pl.ds(pl.multiple_of(at * L, L), L)
        return G.at[u, pl.ds(H + z0, n), :, :, c, :, span]

    def along(axis, at):
        return place(x, at, z, c) if axis == 0 else place(at, y, z, c)

    mine = (y, x)

    def step_b(u):
        for half in range(2):
            drain(G.at[u, 0:H, 0, 0, 0, :, 0 : 3 * L], p1r.at[u, half])
        for axis in range(2):
            ref = wide(u, axis, mine[axis], 0, H)
            for way, step in enumerate((1, -1)):
                remote(
                    ref, ref, p2s.at[u, axis, way], p2r.at[u, axis, way],
                    along(axis, wrap4(mine[axis] + step)),
                ).start()

    def step_c(u):
        for axis in range(2):
            for way, step in enumerate((1, -1)):
                drain(wide(u, axis, mine[axis], 0, H), p2r.at[u, axis, way])
                ref = wide(u, axis, wrap4(mine[axis] - step), way * Q, Q)
                remote(
                    ref, ref, p3s.at[u, axis, way], p3r.at[u, axis, way],
                    along(axis, wrap4(mine[axis] + step)),
                ).start()

    def step_d(u):
        for axis in range(2):
            for way in range(2):
                drain(wide(u, axis, mine[axis], 0, Q), p3r.at[u, axis, way])
        ref = G.at[u, :, :, :, c]
        remote(ref, ref, ss.at[u], sr.at[u], sibling).start()

    def step_e(u):
        drain(G.at[u, :, :, :, c], sr.at[u])

    lane = lax.broadcasted_iota(jnp.int32, (1, 128), 1) // 32
    head_f32 = [(lane == h).astype(F32) for h in range(4)]
    head_bf16 = [mask.astype(BF16) for mask in head_f32]

    def project_qkv(u, rows):
        @pl.loop(0, 4)
        def _(i):
            w = G[u, pl.ds(i * (Z // 4), Z // 4)].reshape(Z // 2, 4, 16, D)[:, 0:3]
            r = dot_nt(xn[0:rows], w.reshape(Z // 2 * 48, D)).astype(BF16)
            for j in range(3):
                qkv[i * 3 + j, 0:rows] = r[:, 128 * j : 128 * j + 128]

    def attend(start, n, bias):
        rows = pl.ds(start, n)

        @pl.loop(0, 4)
        def _(g):
            q, k, v = qkv[g, rows], qkv[4 + g, rows], qkv[8 + g, rows]
            stacked = jnp.concatenate([q * mask for mask in head_bf16], axis=0)
            scores = dot_nt(stacked, k) * 32 ** (-0.5)
            if bias is not None:
                scores = scores + bias
            weights = jnp.exp(scores - jnp.max(scores, axis=-1, keepdims=True)).astype(BF16)
            both = dot(weights, jnp.concatenate([v, jnp.ones_like(v)], axis=1))
            total = head_f32[0] * both[0:n]  [:, 0:128]
            norm = head_f32[0] * both[0:n][:, 128:256]
            for h in range(1, 4):
                part = both[h * n : (h + 1) * n]
                total += head_f32[h] * part[:, 0:128]
                norm += head_f32[h] * part[:, 128:256]
            mix[g, rows] = (total / norm).astype(BF16)

    def project_out(u, rows):
        w = G[u].reshape(2 * Z, 4, 16, D)[:, 3].reshape(D, D)
        mixed = jnp.concatenate([mix[g, 0:rows] for g in range(4)], axis=1)
        return dot_nt(mixed, w)

    def exchange(k, src, dst, devices):
        copies = []
        for i, (start, n) in enumerate(EDGES):
            ref, to = src.at[pl.ds(start, n)], dst.at[pl.ds(start, n)]
            copies.append(remote(ref, to, hs.at[k, i], hr.at[k, i], devices[i]))
            copies[-1].start()
        return copies

    zsend(0)
    for u in range(1, UNITS):
        zsend(u)
    xn[0:ROWS1] = normalize(x_ref[...].astype(F32))
    step_a(0)
    step_b(0)
    step_a(1)
    step_c(0)
    step_b(1)
    step_d(0)
    step_a(2)
    step_c(1)
    step_e(0)
    project_qkv(0, ROWS1)
    step_b(2)
    step_d(1)
    attend(0, 144, None)
    step_a(3)
    step_c(2)
    attend(144, 144, None)
    step_b(3)
    first[...] = (x_ref[...].astype(F32) + project_out(0, ROWS1)).astype(BF16)
    for load in loads:
        load.wait()
    msg_out[...] = dot(p_send[...], first[...]).astype(BF16)
    halo = exchange(0, msg_out, msg_in, halo_down)
    step_d(2)
    step_c(3)
    kept = dot(p_own[...], first[...])
    for copy in halo:
        copy.wait()
    second[...] = (kept + dot(p_arrive[...], msg_in[...])).astype(BF16)
    xn[...] = normalize(second[...].astype(F32))
    step_e(1)
    step_d(3)
    project_qkv(1, ROWS2)
    last = (lat == lats - 1).astype(F32)
    for group in range(4):
        bias = bias_ref[0]
        if group >= 2:
            bias = bias + last * bias_ref[1]
        attend(group * GROUP, GROUP, jnp.concatenate([bias] * 4, axis=0))
    second[...] = (second[...].astype(F32) + project_out(1, ROWS2)).astype(BF16)
    ret_out[...] = dot(p_back[...], second[...]).astype(BF16)
    halo = exchange(1, ret_out, ret_in, halo_up)
    kept = dot(p_qown[...], second[...])
    for copy in halo:
        copy.wait()
    quads = kept + dot(p_qedge[...], ret_in[...])
    quads = jnp.concatenate([quads[GROUP * p : GROUP * (p + 1)] for p in range(4)], axis=1)
    quads = normalize(quads)
    step_e(2)
    step_e(3)
    merged = jnp.zeros((GROUP, 2 * D), F32)
    for p in range(4):
        w = G[2 + p // 2].reshape(2 * Z, 2, 32, D)[:, p % 2].reshape(2 * D, D)
        merged += dot_nt(quads[:, p * D : (p + 1) * D], w)
    out_ref[...] = merged[0:72].astype(BF16)

    for u in range(UNITS):
        drain(G.at[u, 0 : Z - 1, yh, yl, c, :, lanes], zs.at[u])
        for half in range(2):
            drain(G.at[u, 0:H, 0, 0, 0, :, 0 : 3 * L], p1s.at[u, half])
        for axis in range(2):
            for way in range(2):
                drain(wide(u, axis, mine[axis], 0, H), p2s.at[u, axis, way])
                drain(wide(u, axis, mine[axis], 0, Q), p3s.at[u, axis, way])
        drain(G.at[u, :, :, :, c], ss.at[u])


def call(tokens, columns):
    perms = permutations()
    vmem = pl.BlockSpec(memory_space=pltpu.VMEM)
    hbm = pl.BlockSpec(memory_space=pl.ANY)
    dma = pltpu.SemaphoreType.DMA
    return pl.pallas_call(
        kernel,
        out_shape=jax.ShapeDtypeStruct((72, 2 * D), BF16),
        in_specs=[vmem] * 3 + [hbm] * 6,
        out_specs=vmem,
        scratch_shapes=[
            pltpu.VMEM((UNITS, Z, 2, 2, 2, 16, D), BF16),
            pltpu.VMEM((2, 64, D), F32),
            pltpu.VMEM((UNITS, 4, 16, L), BF16),
            pltpu.VMEM((12, ROWS2, 128), BF16),
            pltpu.VMEM((4, ROWS2, 128), BF16),
            pltpu.VMEM((ROWS1, D), BF16),
            pltpu.VMEM((ROWS2, D), BF16),
            pltpu.VMEM((ROWS2, D), BF16),
            pltpu.VMEM((MSG, D), BF16),
            pltpu.VMEM((MSG, D), BF16),
            pltpu.VMEM((MSG, D), BF16),
            pltpu.VMEM((MSG, D), BF16),
        ]
        + [pltpu.VMEM(p.shape, BF16) for p in perms]
        + [
            dma((6,)), dma((UNITS,)), dma(()), dma(()), dma((UNITS,)), dma((UNITS,)),
            dma((UNITS, 2)), dma((UNITS, 2)),
            dma((UNITS, 2, 2)), dma((UNITS, 2, 2)), dma((UNITS, 2, 2)), dma((UNITS, 2, 2)),
            dma((UNITS,)), dma((UNITS,)), dma((2, 3)), dma((2, 3)),
        ],
        compiler_params=pltpu.CompilerParams(
            collective_id=0, has_side_effects=True, vmem_limit_bytes=48 * 1024 * 1024
        ),
        name="swin",
    )(tokens, columns, biases(), *perms)


def body(patches, qkv_first, proj_first, qkv_second, proj_second, merge_weight):
    tokens = patches.reshape(12, 2, 6, 2, D).transpose(1, 0, 2, 3, 4).reshape(ROWS1, D)
    merge = [merge_weight[p * D : (p + 1) * D] for p in range(4)]
    columns = jnp.concatenate([qkv_first, proj_first, qkv_second, proj_second] + merge, axis=1)
    merged = call(tokens, columns)
    return merged.reshape(6, 6, 2, 2 * D)


def solution(mesh):
    placed = (
        P("lon", "lat", None, None),
        P(None, "lon"),
        P(None, "lon"),
        P(None, "lon"),
        P(None, "lon"),
        P(None, "lon"),
    )
    return jax.shard_map(
        body, mesh=mesh, in_specs=placed, out_specs=P("lon", "lat", None, None), check_vma=False
    )
```

```python
import functools

import jax
import jax.numpy as jnp
from jax import lax
from jax.experimental import pallas as pl
from jax.experimental.pallas import tpu as pltpu
from jax.sharding import PartitionSpec as P

D = 512
HEADS = 16
Z = 16
H = Z // 2
Q = H // 2
L = D // 4
SLABS = 4
UNITS = ((0, 1), (1, 1), (2, 2))
ROWS1 = 288
GROUP = 80
ROWS2 = 4 * GROUP
MSG = 208
EDGES = ((0, 112), (112, 48), (160, 48))
norm_epsilon = 1e-05
masked_score = -1e30
EXP2_SCALE = 32 ** (-0.5) * 1.4426950408889634
MESH = pl.DeviceIdType.MESH
F32 = jnp.float32
BF16 = jnp.bfloat16


def split(values, n):
    quotient = jnp.floor((values + 0.5) * (1.0 / n))
    return quotient, values - n * quotient


def both(*conditions):
    return functools.reduce(jnp.logical_and, conditions)


def edge_row(lo, la, lv):
    near = jnp.where(lo < 6, 160 + (lo * 3 + la) * 2 + lv, 112 + ((lo - 6) * 3 + la) * 2 + lv)
    return jnp.where(both(lo < 6, la >= 3), (lo * 9 + la - 3) * 2 + lv, near)


def first_row(lo, la, lv):
    window, rest = split(la, 6)
    return window * 144 + lo * 12 + rest * 2 + lv


def shifted_row(lo, la, lv):
    window, rest = split(jnp.where(la < 3, la + 9, la - 3), 6)
    return (window * 2 + lv) * GROUP + jnp.where(lo < 6, lo + 6, lo - 6) * 6 + rest


def edge_tokens(row):
    start = jnp.where(row < 112, 0, jnp.where(row < 160, 112, 160))
    half, lv = split(row - start, 2)
    lo9, la9 = split(half, 9)
    lo3, la3 = split(half, 3)
    wide = row < 112
    lo = jnp.where(wide, lo9, jnp.where(row < 160, lo3 + 6, lo3))
    la = jnp.where(wide, la9 + 3, la3)
    return lo, la, lv, half < jnp.where(wide, 54, 18)


def shifted_tokens(row):
    group, place = split(row, GROUP)
    window, lv = split(group, 2)
    slo, sla = split(place, 6)
    la = window * 6 + sla + 3
    lo = jnp.where(slo < 6, slo + 6, slo - 6)
    return lo, jnp.where(la < 12, la, la - 12), lv, place < 72


def quad_tokens(row):
    part, place = split(row, GROUP)
    odd_lat, odd_lon = split(part, 2)
    half, lv = split(place, 2)
    i, j = split(half, 6)
    return 2 * i + odd_lon, 2 * j + odd_lat, lv, place < 72


def one_hot(rows, columns, column_of):
    row = lax.broadcasted_iota(jnp.int32, (rows, 1), 0).astype(F32)
    at, valid = column_of(row)
    at = jnp.where(valid, at, -1.0)
    column = lax.broadcasted_iota(jnp.int32, (rows, columns), 1).astype(F32)
    return jnp.where(column == at, 1.0, 0.0).astype(BF16)


def column_send(row):
    lo, la, lv, valid = edge_tokens(row)
    return first_row(lo, la, lv), valid


def column_back(row):
    lo, la, lv, valid = edge_tokens(row)
    return shifted_row(lo, la, lv), valid


def kept(lo, la):
    return both(lo >= 6, la >= 3)


def column_own(row):
    lo, la, lv, valid = shifted_tokens(row)
    return first_row(lo, la, lv), both(valid, kept(lo, la))


def column_arrive(row):
    lo, la, lv, valid = shifted_tokens(row)
    return edge_row(lo, la, lv), both(valid, jnp.logical_not(kept(lo, la)))


def column_quad_own(row):
    lo, la, lv, valid = quad_tokens(row)
    return shifted_row(lo, la, lv), both(valid, kept(lo, la))


def column_quad_edge(row):
    lo, la, lv, valid = quad_tokens(row)
    return edge_row(lo, la, lv), both(valid, jnp.logical_not(kept(lo, la)))


PERMUTATIONS = (
    (MSG, ROWS1, column_send),
    (ROWS2, ROWS1, column_own),
    (ROWS2, MSG, column_arrive),
    (MSG, ROWS2, column_back),
    (4 * GROUP, ROWS2, column_quad_own),
    (4 * GROUP, MSG, column_quad_edge),
)


def normalize(values):
    centred = values - jnp.mean(values, axis=-1, keepdims=True)
    variance = jnp.mean(centred * centred, axis=-1, keepdims=True)
    return (centred * lax.rsqrt(variance + norm_epsilon)).astype(BF16)


def dot_nt(a, b):
    return lax.dot_general(a, b, (((1,), (1,)), ((), ())), preferred_element_type=F32)


def dot(a, b):
    return jnp.dot(a, b, preferred_element_type=F32)


def kernel(
    x_ref, q1_hbm, o1_hbm, q2_hbm, o2_hbm, merge_hbm, out_ref,
    G, E, piece, qkv, mix, first, second, xn, msg_out, msg_in, ret_out, ret_in,
    p_send, p_own, p_arrive, p_back, p_qown, p_qedge, bias_ref, q1, o1, q2, o2, merge,
    wsem, lsem, es, er, zs, zr, p1s, p1r, p2s, p2r, p3s, p3r, ss, sr, hs, hr,
):
    lon, lat = lax.axis_index("lon"), lax.axis_index("lat")
    lons, lats = 4 * Z, 8
    c = lax.rem(lon, 2)
    yh = lax.rem(lon // 2, 2)
    z = lon // 4
    x = lax.rem(lat, 4)
    yl = lat // 4
    y = yh * 2 + yl
    lanes = pl.ds(pl.multiple_of(x * L, L), L)

    def place(x, y, z, c):
        return ((z * 2 + y // 2) * 2 + c, lax.rem(y, 2) * 4 + x)

    def wrap4(v):
        return lax.rem(v + 4, 4)

    sibling = place(x, y, z, 1 - c)
    lon_up, lon_down = lax.rem(lon + 1, lons), lax.rem(lon + lons - 1, lons)
    lat_up, lat_down = lax.rem(lat + 1, lats), lax.rem(lat + lats - 1, lats)
    halo_down = ((lon_down, lat), (lon, lat_down), (lon_down, lat_down))
    halo_up = ((lon_up, lat), (lon, lat_up), (lon_up, lat_up))

    def remote(src, dst, send, recv, device):
        return pltpu.make_async_remote_copy(
            src_ref=src, dst_ref=dst, send_sem=send, recv_sem=recv,
            device_id=device, device_id_type=MESH,
        )

    def drain(ref, sem):
        pltpu.make_async_copy(ref, ref, sem).wait()

    own_columns = ((q1_hbm, q1), (o1_hbm, o1), (q2_hbm, q2), (o2_hbm, o2), (merge_hbm, merge))
    loads = [
        pltpu.make_async_copy(src, dst, wsem.at[i]) for i, (src, dst) in enumerate(own_columns)
    ]
    for load in loads:
        load.start()

    barrier = pltpu.get_barrier_semaphore()

    def greet(device):
        pl.semaphore_signal(barrier, inc=1, device_id=device, device_id_type=MESH)

    def distance(k):
        return 8 + (1 - 2 * lax.rem(k + 1, 2)) * ((k + 1) // 2)

    @pl.loop(0, Z - 1)
    def _(k):
        greet(place(x, y, lax.rem(z + distance(k), Z), c))

    for d in (2, 1, 3):
        greet(place(wrap4(x + d), y, z, c))
        greet(place(x, wrap4(y + d), z, c))
    for device in halo_down + halo_up:
        greet(device)
    greet(sibling)

    for load in loads:
        load.wait()
    for ref, start, n in ((q1, 0, 24), (o1, 24, 8), (q2, 32, 24), (o2, 56, 8)):
        E[c, start : start + n] = ref[...].astype(F32)
    pl.semaphore_wait(barrier, 1 + Z - 1 + 6 + 6)
    to_sibling = remote(E.at[c], E.at[c], es, er, sibling)
    to_sibling.start()

    low, high = (yl == 0).astype(F32), (yl == 1).astype(F32)
    core0, core1 = (c == 0).astype(F32), (c == 1).astype(F32)

    def put_piece(u, tile):
        tile = tile.astype(BF16)
        for k in range(4):
            piece[u, k] = tile[:, k * L : (k + 1) * L]

    for m in range(2):
        rows = merge[:, 2 * m * D : 2 * (m + 1) * D].astype(F32)
        put_piece(2 + m, rows[:, 0:D] * low + rows[:, D : 2 * D] * high)
    to_sibling.wait()
    for s in range(2):
        r0, r1 = E[0, 32 * s : 32 * s + 32], E[1, 32 * s : 32 * s + 32]
        tile = (low * core0) * r0[0:16]
        tile += (low * core1) * jnp.concatenate([r0[16:24], r1[0:8]], axis=0)
        tile += (high * core0) * r1[8:24]
        tile += (high * core1) * jnp.concatenate([r0[24:32], r1[24:32]], axis=0)
        put_piece(s, tile)

    def of(u):
        return pl.ds(*UNITS[u])

    def home(u):
        return G.at[of(u), z, yh, yl, c, :, lanes]

    def zsend(u):
        src, slot = piece.at[of(u), x], home(u)
        pltpu.make_async_copy(src, slot, lsem.at[u]).start()

        @pl.loop(0, Z - 1)
        def _(k):
            device = place(x, y, lax.rem(z + distance(k), Z), c)
            remote(src, slot, zs.at[u], zr.at[u], device).start()

    def zbytes(u):
        return G.at[of(u), 0 : Z - 1, yh, yl, c, :, lanes]

    def p1bytes(u):
        return G.at[of(u), 0:H, 0, 0, 0, :, 0 : 3 * L]

    def step_a(u):
        pltpu.make_async_copy(piece.at[of(u), x], home(u), lsem.at[u]).wait()
        drain(zbytes(u), zr.at[u])
        half0 = G.at[of(u), 0:H, yh, yl, c, :, lanes]
        half1 = G.at[of(u), H:Z, yh, yl, c, :, lanes]
        for d in (2, 1, 3):
            remote(half0, half0, p1s.at[u, 0], p1r.at[u, 0], place(wrap4(x + d), y, z, c)).start()
            remote(half1, half1, p1s.at[u, 1], p1r.at[u, 1], place(x, wrap4(y + d), z, c)).start()

    def wide(u, axis, at, z0, n):
        if axis == 0:
            return G.at[of(u), pl.ds(z0, n), at // 2, lax.rem(at, 2), c]
        span = pl.ds(pl.multiple_of(at * L, L), L)
        return G.at[of(u), pl.ds(H + z0, n), :, :, c, :, span]

    def along(axis, at):
        return place(x, at, z, c) if axis == 0 else place(at, y, z, c)

    mine = (y, x)

    def to_core(u, axis, at):
        ref = wide(u, axis, at, 0, H)
        remote(ref, ref, ss.at[u], sr.at[u], sibling).start()

    def step_b(u):
        for axis in range(2):
            drain(p1bytes(u), p1r.at[u, axis])
            ref = wide(u, axis, mine[axis], 0, H)
            for way, step in enumerate((1, -1)):
                remote(
                    ref, ref, p2s.at[u, axis, way], p2r.at[u, axis, way],
                    along(axis, wrap4(mine[axis] + step)),
                ).start()
        if u == 0:
            for axis in range(2):
                to_core(u, axis, mine[axis])

    def step_c(u):
        for axis in range(2):
            for way, step in enumerate((1, -1)):
                drain(wide(u, axis, mine[axis], 0, H), p2r.at[u, axis, way])
                ref = wide(u, axis, wrap4(mine[axis] - step), way * Q, Q)
                remote(
                    ref, ref, p3s.at[u, axis, way], p3r.at[u, axis, way],
                    along(axis, wrap4(mine[axis] + step)),
                ).start()
        if u == 0:
            for axis in range(2):
                for step in (1, -1):
                    to_core(u, axis, wrap4(mine[axis] + step))

    def step_d(u):
        for axis in range(2):
            for way in range(2):
                drain(wide(u, axis, mine[axis], 0, Q), p3r.at[u, axis, way])
            if u == 0:
                to_core(u, axis, wrap4(mine[axis] + 2))
        if u > 0:
            ref = G.at[of(u), :, :, :, c]
            remote(ref, ref, ss.at[u], sr.at[u], sibling).start()

    def step_e(u):
        drain(G.at[of(u), :, :, :, c], sr.at[u])

    lane = lax.broadcasted_iota(jnp.int32, (1, 128), 1) // 32
    head_f32 = [(lane == h).astype(F32) for h in range(4)]
    head_bf16 = [mask.astype(BF16) for mask in head_f32]

    def project_qkv(u, rows):
        @pl.loop(0, 4)
        def _(i):
            w = G[u, pl.ds(i * (Z // 4), Z // 4)].reshape(Z // 2, 4, 16, D)[:, 0:3]
            r = dot_nt(xn[0:rows], w.reshape(Z // 2 * 48, D)).astype(BF16)
            for j in range(3):
                qkv[i * 3 + j, 0:rows] = r[:, 128 * j : 128 * j + 128]

    def attend(start, n, bias):
        rows = pl.ds(start, n)
        for g in range(4):
            q, k, v = qkv[g, rows], qkv[4 + g, rows], qkv[8 + g, rows]
            stacked = jnp.concatenate([q * mask for mask in head_bf16], axis=0)
            scores = dot_nt(stacked, k)
            if bias is not None:
                scores = scores + bias
            highest = jnp.max(scores, axis=-1, keepdims=True)
            weights = jnp.exp2((scores - highest) * EXP2_SCALE).astype(BF16)
            summed = dot(weights, jnp.concatenate([v, jnp.ones_like(v)], axis=1))
            total = head_f32[0] * summed[0:n, 0:128]
            norm = head_f32[0] * summed[0:n, 128:256]
            for h in range(1, 4):
                total += head_f32[h] * summed[h * n : (h + 1) * n, 0:128]
                norm += head_f32[h] * summed[h * n : (h + 1) * n, 128:256]
            mix[g, rows] = (total / norm).astype(BF16)

    def project_out(u, rows):
        w = G[u].reshape(2 * Z, 4, 16, D)[:, 3].reshape(D, D)
        mixed = jnp.concatenate([mix[g, 0:rows] for g in range(4)], axis=1)
        return dot_nt(mixed, w)

    def exchange(k, src, dst, devices):
        copies = []
        for i, (start, n) in enumerate(EDGES):
            ref, to = src.at[pl.ds(start, n)], dst.at[pl.ds(start, n)]
            copies.append(remote(ref, to, hs.at[k, i], hr.at[k, i], devices[i]))
            copies[-1].start()
        return copies

    zsend(0)
    for ref, (rows, columns, column_of) in zip(
        (p_send, p_own, p_arrive, p_back, p_qown, p_qedge), PERMUTATIONS
    ):
        ref[...] = one_hot(rows, columns, column_of)
    row = lax.broadcasted_iota(jnp.int32, (GROUP, GROUP), 0).astype(F32)
    column = lax.broadcasted_iota(jnp.int32, (GROUP, GROUP), 1).astype(F32)
    bias_ref[0] = jnp.where(column < 72, 0.0, masked_score)
    north = split(row, 6)[1] < 3
    bias_ref[1] = jnp.where(north == (split(column, 6)[1] < 3), 0.0, masked_score)
    xn[0:ROWS1] = normalize(x_ref[...].astype(F32))
    step_a(0)
    zsend(1)
    zsend(2)
    step_b(0)
    step_c(0)
    step_a(1)
    step_d(0)
    step_b(1)
    step_a(2)
    step_e(0)
    project_qkv(0, ROWS1)
    attend(0, 144, None)
    step_c(1)
    attend(144, 144, None)
    step_b(2)
    first[...] = (x_ref[...].astype(F32) + project_out(0, ROWS1)).astype(BF16)
    msg_out[...] = dot(p_send[...], first[...]).astype(BF16)
    halo_first = exchange(0, msg_out, msg_in, halo_down)
    stay = dot(p_own[...], first[...])
    step_d(1)
    for copy in halo_first:
        copy.wait_recv()
    second[...] = (stay + dot(p_arrive[...], msg_in[...])).astype(BF16)
    xn[...] = normalize(second[...].astype(F32))
    step_e(1)
    project_qkv(1, ROWS2)
    step_c(2)
    last = (lat == lats - 1).astype(F32)

    def attend_shifted(group):
        bias = bias_ref[0] + (last * (group >= 2).astype(F32)) * bias_ref[1]
        attend(pl.multiple_of(group * GROUP, 16), GROUP, jnp.concatenate([bias] * 4, axis=0))

    pl.loop(0, 4)(attend_shifted)
    step_d(2)
    second[...] = (second[...].astype(F32) + project_out(1, ROWS2)).astype(BF16)
    ret_out[...] = dot(p_back[...], second[...]).astype(BF16)
    halo_second = exchange(1, ret_out, ret_in, halo_up)
    stay = dot(p_qown[...], second[...])
    for copy in halo_second:
        copy.wait_recv()
    quads = stay + dot(p_qedge[...], ret_in[...])
    quads = jnp.concatenate([quads[GROUP * p : GROUP * (p + 1)] for p in range(4)], axis=1)
    quads = normalize(quads)
    step_e(2)
    merged = jnp.zeros((GROUP, 2 * D), F32)
    for p in range(4):
        w = G[2 + p // 2].reshape(2 * Z, 2, 32, D)[:, p % 2].reshape(2 * D, D)
        merged += dot_nt(quads[:, p * D : (p + 1) * D], w)
    out_ref[...] = merged[0:72].astype(BF16)

    for copy in halo_first + halo_second:
        copy.wait_send()
    for u in range(len(UNITS)):
        drain(zbytes(u), zs.at[u])
        for axis in range(2):
            drain(p1bytes(u), p1s.at[u, axis])
            for way in range(2):
                drain(wide(u, axis, mine[axis], 0, H), p2s.at[u, axis, way])
                drain(wide(u, axis, mine[axis], 0, Q), p3s.at[u, axis, way])
        drain(G.at[of(u), :, :, :, c], ss.at[u])


def call(tokens, *columns):
    vmem = pl.BlockSpec(memory_space=pltpu.VMEM)
    dma = pltpu.SemaphoreType.DMA
    return pl.pallas_call(
        kernel,
        out_shape=jax.ShapeDtypeStruct((72, 2 * D), BF16),
        in_specs=[vmem] + [pl.BlockSpec(memory_space=pl.ANY)] * 5,
        out_specs=vmem,
        scratch_shapes=[
            pltpu.VMEM((SLABS, Z, 2, 2, 2, 16, D), BF16),
            pltpu.VMEM((2, 64, D), F32),
            pltpu.VMEM((SLABS, 4, 16, L), BF16),
            pltpu.VMEM((12, ROWS2, 128), BF16),
            pltpu.VMEM((4, ROWS2, 128), BF16),
            pltpu.VMEM((ROWS1, D), BF16),
            pltpu.VMEM((ROWS2, D), BF16),
            pltpu.VMEM((ROWS2, D), BF16),
            pltpu.VMEM((MSG, D), BF16),
            pltpu.VMEM((MSG, D), BF16),
            pltpu.VMEM((MSG, D), BF16),
            pltpu.VMEM((MSG, D), BF16),
        ]
        + [pltpu.VMEM(p[:2], BF16) for p in PERMUTATIONS]
        + [
            pltpu.VMEM((2, GROUP, GROUP), F32),
            pltpu.VMEM((24, D), BF16),
            pltpu.VMEM((8, D), BF16),
            pltpu.VMEM((24, D), BF16),
            pltpu.VMEM((8, D), BF16),
            pltpu.VMEM((16, 4 * D), BF16),
            dma((5,)),
            dma((len(UNITS),)), dma(()), dma(()), dma((len(UNITS),)), dma((len(UNITS),)),
            dma((len(UNITS), 2)), dma((len(UNITS), 2)),
            dma((len(UNITS), 2, 2)), dma((len(UNITS), 2, 2)), dma((len(UNITS), 2, 2)), dma((len(UNITS), 2, 2)),
            dma((len(UNITS),)), dma((len(UNITS),)), dma((2, 3)), dma((2, 3)),
        ],
        compiler_params=pltpu.CompilerParams(
            collective_id=0, has_side_effects=True, vmem_limit_bytes=48 * 1024 * 1024
        ),
        name="swin",
    )(tokens, *columns)


def body(patches, qkv_first, proj_first, qkv_second, proj_second, merge_weight):
    tokens = patches.reshape(12, 2, 6, 2, D).transpose(1, 0, 2, 3, 4).reshape(ROWS1, D)
    merged = call(
        tokens, qkv_first.T, proj_first.T, qkv_second.T, proj_second.T, merge_weight.T
    )
    return merged.reshape(6, 6, 2, 2 * D)


def solution(mesh):
    placed = (
        P("lon", "lat", None, None),
        P(None, "lon"),
        P(None, "lon"),
        P(None, "lon"),
        P(None, "lon"),
        P(None, "lon"),
    )
    return jax.shard_map(
        body, mesh=mesh, in_specs=placed, out_specs=P("lon", "lat", None, None), check_vma=False
    )
```

```python
import functools

import jax
import jax.numpy as jnp
from jax import lax
from jax.experimental import pallas as pl
from jax.experimental.pallas import tpu as pltpu
from jax.sharding import PartitionSpec as P

D = 512
HEADS = 16
Z = 16
H = Z // 2
Q = H // 2
L = D // 4
SLABS = 4
UNITS = ((0, 1), (1, 1), (2, 2))
DIRECT = (True, False, False)
WAYS = ((0, 1), (1, -1), (2, 2))
ROWS1 = 288
GROUP = 80
ROWS2 = 4 * GROUP
MSG = 208
EDGES = ((0, 112), (112, 48), (160, 48))
norm_epsilon = 1e-05
masked_score = -1e30
EXP2_SCALE = 32 ** (-0.5) * 1.4426950408889634
MESH = pl.DeviceIdType.MESH
F32 = jnp.float32
BF16 = jnp.bfloat16


def split(values, n):
    quotient = jnp.floor((values + 0.5) * (1.0 / n))
    return quotient, values - n * quotient


def both(*conditions):
    return functools.reduce(jnp.logical_and, conditions)


def edge_row(lo, la, lv):
    near = jnp.where(lo < 6, 160 + (lo * 3 + la) * 2 + lv, 112 + ((lo - 6) * 3 + la) * 2 + lv)
    return jnp.where(both(lo < 6, la >= 3), (lo * 9 + la - 3) * 2 + lv, near)


def first_row(lo, la, lv):
    window, rest = split(la, 6)
    return window * 144 + lo * 12 + rest * 2 + lv


def shifted_row(lo, la, lv):
    window, rest = split(jnp.where(la < 3, la + 9, la - 3), 6)
    return (window * 2 + lv) * GROUP + jnp.where(lo < 6, lo + 6, lo - 6) * 6 + rest


def edge_tokens(row):
    start = jnp.where(row < 112, 0, jnp.where(row < 160, 112, 160))
    half, lv = split(row - start, 2)
    lo9, la9 = split(half, 9)
    lo3, la3 = split(half, 3)
    wide = row < 112
    lo = jnp.where(wide, lo9, jnp.where(row < 160, lo3 + 6, lo3))
    la = jnp.where(wide, la9 + 3, la3)
    return lo, la, lv, half < jnp.where(wide, 54, 18)


def shifted_tokens(row):
    group, place = split(row, GROUP)
    window, lv = split(group, 2)
    slo, sla = split(place, 6)
    la = window * 6 + sla + 3
    lo = jnp.where(slo < 6, slo + 6, slo - 6)
    return lo, jnp.where(la < 12, la, la - 12), lv, place < 72


def quad_tokens(row):
    part, place = split(row, GROUP)
    odd_lat, odd_lon = split(part, 2)
    half, lv = split(place, 2)
    i, j = split(half, 6)
    return 2 * i + odd_lon, 2 * j + odd_lat, lv, place < 72


def one_hot(rows, columns, column_of):
    row = lax.broadcasted_iota(jnp.int32, (rows, 1), 0).astype(F32)
    at, valid = column_of(row)
    at = jnp.where(valid, at, -1.0)
    column = lax.broadcasted_iota(jnp.int32, (rows, columns), 1).astype(F32)
    return jnp.where(column == at, 1.0, 0.0).astype(BF16)


def column_send(row):
    lo, la, lv, valid = edge_tokens(row)
    return first_row(lo, la, lv), valid


def column_back(row):
    lo, la, lv, valid = edge_tokens(row)
    return shifted_row(lo, la, lv), valid


def kept(lo, la):
    return both(lo >= 6, la >= 3)


def column_own(row):
    lo, la, lv, valid = shifted_tokens(row)
    return first_row(lo, la, lv), both(valid, kept(lo, la))


def column_arrive(row):
    lo, la, lv, valid = shifted_tokens(row)
    return edge_row(lo, la, lv), both(valid, jnp.logical_not(kept(lo, la)))


def column_quad_own(row):
    lo, la, lv, valid = quad_tokens(row)
    return shifted_row(lo, la, lv), both(valid, kept(lo, la))


def column_quad_edge(row):
    lo, la, lv, valid = quad_tokens(row)
    return edge_row(lo, la, lv), both(valid, jnp.logical_not(kept(lo, la)))


PERMUTATIONS = (
    (MSG, ROWS1, column_send),
    (ROWS2, ROWS1, column_own),
    (ROWS2, MSG, column_arrive),
    (MSG, ROWS2, column_back),
    (4 * GROUP, ROWS2, column_quad_own),
    (4 * GROUP, MSG, column_quad_edge),
)


def normalize(values):
    centred = values - jnp.mean(values, axis=-1, keepdims=True)
    variance = jnp.mean(centred * centred, axis=-1, keepdims=True)
    return (centred * lax.rsqrt(variance + norm_epsilon)).astype(BF16)


def dot_nt(a, b):
    return lax.dot_general(a, b, (((1,), (1,)), ((), ())), preferred_element_type=F32)


def dot(a, b):
    return jnp.dot(a, b, preferred_element_type=F32)


def kernel(
    x_hbm, q1_hbm, o1_hbm, q2_hbm, o2_hbm, merge_hbm, out_ref,
    G, E, piece, qkv, mix, first, second, xn, msg_out, msg_in, ret_out, ret_in,
    p_send, p_own, p_arrive, p_back, p_qown, p_qedge, bias_ref, q1, o1, q2, o2, merge, grid, x_ref,
    wsem, lsem, es, er, zs, zr, p1s, p1r, p2s, p2r, p3s, p3r, ss, sr, hs, hr,
):
    lon, lat = lax.axis_index("lon"), lax.axis_index("lat")
    lons, lats = 4 * Z, 8
    c = lax.rem(lon, 2)
    yh = lax.rem(lon // 2, 2)
    z = lon // 4
    x = lax.rem(lat, 4)
    yl = lat // 4
    y = yh * 2 + yl
    lanes = pl.ds(pl.multiple_of(x * L, L), L)

    def place(x, y, z, c):
        return ((z * 2 + y // 2) * 2 + c, lax.rem(y, 2) * 4 + x)

    def wrap4(v):
        return lax.rem(v + 4, 4)

    sibling = place(x, y, z, 1 - c)
    lon_up, lon_down = lax.rem(lon + 1, lons), lax.rem(lon + lons - 1, lons)
    lat_up, lat_down = lax.rem(lat + 1, lats), lax.rem(lat + lats - 1, lats)
    halo_down = ((lon_down, lat), (lon, lat_down), (lon_down, lat_down))
    halo_up = ((lon_up, lat), (lon, lat_up), (lon_up, lat_up))

    def remote(src, dst, send, recv, device):
        return pltpu.make_async_remote_copy(
            src_ref=src, dst_ref=dst, send_sem=send, recv_sem=recv,
            device_id=device, device_id_type=MESH,
        )

    def drain(ref, sem):
        pltpu.make_async_copy(ref, ref, sem).wait()

    own_columns = ((q1_hbm, q1), (o1_hbm, o1), (q2_hbm, q2), (o2_hbm, o2), (merge_hbm, merge))
    grid_load = pltpu.make_async_copy(x_hbm, grid, wsem.at[5])
    grid_load.start()
    loads = [
        pltpu.make_async_copy(src, dst, wsem.at[i]) for i, (src, dst) in enumerate(own_columns)
    ]
    for load in loads:
        load.start()

    barrier = pltpu.get_barrier_semaphore()

    def greet(device):
        pl.semaphore_signal(barrier, inc=1, device_id=device, device_id_type=MESH)

    def distance(k):
        return 8 + (1 - 2 * lax.rem(k + 1, 2)) * ((k + 1) // 2)

    @pl.loop(0, Z - 1)
    def _(k):
        greet(place(x, y, lax.rem(z + distance(k), Z), c))

    for d in (2, 1, 3):
        greet(place(wrap4(x + d), y, z, c))
        greet(place(x, wrap4(y + d), z, c))
    for device in halo_down + halo_up:
        greet(device)
    greet(sibling)

    for load in loads:
        load.wait()
    for ref, start, n in ((q1, 0, 24), (o1, 24, 8), (q2, 32, 24), (o2, 56, 8)):
        E[c, start : start + n] = ref[...].astype(F32)
    pl.semaphore_wait(barrier, 1 + Z - 1 + 6 + 6)
    to_sibling = remote(E.at[c], E.at[c], es, er, sibling)
    to_sibling.start()

    low, high = (yl == 0).astype(F32), (yl == 1).astype(F32)
    core0, core1 = (c == 0).astype(F32), (c == 1).astype(F32)

    def put_piece(u, tile):
        tile = tile.astype(BF16)
        for k in range(4):
            piece[u, k] = tile[:, k * L : (k + 1) * L]

    for m in range(2):
        rows = merge[:, 2 * m * D : 2 * (m + 1) * D].astype(F32)
        put_piece(2 + m, rows[:, 0:D] * low + rows[:, D : 2 * D] * high)
    to_sibling.wait()
    for s in range(2):
        r0, r1 = E[0, 32 * s : 32 * s + 32], E[1, 32 * s : 32 * s + 32]
        tile = (low * core0) * r0[0:16]
        tile += (low * core1) * jnp.concatenate([r0[16:24], r1[0:8]], axis=0)
        tile += (high * core0) * r1[8:24]
        tile += (high * core1) * jnp.concatenate([r0[24:32], r1[24:32]], axis=0)
        put_piece(s, tile)

    def of(u):
        return pl.ds(*UNITS[u])

    def home(u):
        return G.at[of(u), z, yh, yl, c, :, lanes]

    def zsend(u):
        src, slot = piece.at[of(u), x], home(u)
        pltpu.make_async_copy(src, slot, lsem.at[u]).start()

        @pl.loop(0, Z - 1)
        def _(k):
            device = place(x, y, lax.rem(z + distance(k), Z), c)
            remote(src, slot, zs.at[u], zr.at[u], device).start()

    def zbytes(u):
        return G.at[of(u), 0 : Z - 1, yh, yl, c, :, lanes]

    def p1bytes(u):
        return G.at[of(u), 0:H, 0, 0, 0, :, 0 : 3 * L]

    def step_a(u):
        pltpu.make_async_copy(piece.at[of(u), x], home(u), lsem.at[u]).wait()
        drain(zbytes(u), zr.at[u])
        half0 = G.at[of(u), 0:H, yh, yl, c, :, lanes]
        half1 = G.at[of(u), H:Z, yh, yl, c, :, lanes]
        for d in (2, 1, 3):
            remote(half0, half0, p1s.at[u, 0], p1r.at[u, 0], place(wrap4(x + d), y, z, c)).start()
            remote(half1, half1, p1s.at[u, 1], p1r.at[u, 1], place(x, wrap4(y + d), z, c)).start()

    def wide(u, axis, at, z0, n):
        if axis == 0:
            return G.at[of(u), pl.ds(z0, n), at // 2, lax.rem(at, 2), c]
        span = pl.ds(pl.multiple_of(at * L, L), L)
        return G.at[of(u), pl.ds(H + z0, n), :, :, c, :, span]

    def along(axis, at):
        return place(x, at, z, c) if axis == 0 else place(at, y, z, c)

    mine = (y, x)

    def to_core(u, axis, at):
        ref = wide(u, axis, at, 0, H)
        remote(ref, ref, ss.at[u], sr.at[u], sibling).start()

    def step_b(u):
        for axis in range(2):
            drain(p1bytes(u), p1r.at[u, axis])
            ref = wide(u, axis, mine[axis], 0, H)
            for way, step in WAYS[: 3 if DIRECT[u] else 2]:
                remote(
                    ref, ref, p2s.at[u, axis, way], p2r.at[u, axis, way],
                    along(axis, wrap4(mine[axis] + step)),
                ).start()
        for axis in range(2):
            to_core(u, axis, mine[axis])

    def step_c(u):
        for axis in range(2):
            for way, step in WAYS[:2]:
                drain(wide(u, axis, mine[axis], 0, H), p2r.at[u, axis, way])
                if not DIRECT[u]:
                    ref = wide(u, axis, wrap4(mine[axis] - step), way * Q, Q)
                    remote(
                        ref, ref, p3s.at[u, axis, way], p3r.at[u, axis, way],
                        along(axis, wrap4(mine[axis] + step)),
                    ).start()
        for axis in range(2):
            for way, step in WAYS[:2]:
                to_core(u, axis, wrap4(mine[axis] + step))

    def step_d(u):
        for axis in range(2):
            if DIRECT[u]:
                drain(wide(u, axis, mine[axis], 0, H), p2r.at[u, axis, 2])
            else:
                for way in range(2):
                    drain(wide(u, axis, mine[axis], 0, Q), p3r.at[u, axis, way])
            to_core(u, axis, wrap4(mine[axis] + 2))

    def step_e(u):
        drain(G.at[of(u), :, :, :, c], sr.at[u])

    lane = lax.broadcasted_iota(jnp.int32, (1, 128), 1) // 32
    head_f32 = [(lane == h).astype(F32) for h in range(4)]
    head_bf16 = [mask.astype(BF16) for mask in head_f32]

    def project_qkv(u, rows):
        w = G[u].reshape(2 * Z, 4, 16, D)[:, 0:3].reshape(3 * D, D)
        for i in range(3):
            r = dot_nt(xn[0:rows], w[D * i : D * (i + 1)]).astype(BF16)
            for j in range(4):
                qkv[i * 4 + j, 0:rows] = r[:, 128 * j : 128 * j + 128]

    def attend(start, n, bias):
        rows = pl.ds(start, n)
        for g in range(4):
            q, k, v = qkv[g, rows], qkv[4 + g, rows], qkv[8 + g, rows]
            stacked = jnp.concatenate([q * mask for mask in head_bf16], axis=0)
            scores = dot_nt(stacked, k)
            if bias is not None:
                scores = scores + bias
            highest = jnp.max(scores, axis=-1, keepdims=True)
            weights = jnp.exp2((scores - highest) * EXP2_SCALE).astype(BF16)
            summed = dot(weights, jnp.concatenate([v, jnp.ones_like(v)], axis=1))
            total = head_f32[0] * summed[0:n, 0:128]
            norm = head_f32[0] * summed[0:n, 128:256]
            for h in range(1, 4):
                total += head_f32[h] * summed[h * n : (h + 1) * n, 0:128]
                norm += head_f32[h] * summed[h * n : (h + 1) * n, 128:256]
            mix[g, rows] = (total / norm).astype(BF16)

    def project_out(u, rows):
        w = G[u].reshape(2 * Z, 4, 16, D)[:, 3].reshape(D, D)
        mixed = jnp.concatenate([mix[g, 0:rows] for g in range(4)], axis=1)
        return dot_nt(mixed, w)

    def exchange(k, src, dst, devices):
        copies = []
        for i, (start, n) in enumerate(EDGES):
            ref, to = src.at[pl.ds(start, n)], dst.at[pl.ds(start, n)]
            copies.append(remote(ref, to, hs.at[k, i], hr.at[k, i], devices[i]))
            copies[-1].start()
        return copies

    zsend(0)
    for ref, (rows, columns, column_of) in zip(
        (p_send, p_own, p_arrive, p_back, p_qown, p_qedge), PERMUTATIONS
    ):
        ref[...] = one_hot(rows, columns, column_of)
    row = lax.broadcasted_iota(jnp.int32, (GROUP, GROUP), 0).astype(F32)
    column = lax.broadcasted_iota(jnp.int32, (GROUP, GROUP), 1).astype(F32)
    bias_ref[0] = jnp.where(column < 72, 0.0, masked_score)
    north = split(row, 6)[1] < 3
    bias_ref[1] = jnp.where(north == (split(column, 6)[1] < 3), 0.0, masked_score)
    grid_load.wait()
    for w in range(2):
        x_ref[144 * w : 144 * w + 144] = grid[:, 6 * w : 6 * w + 6].reshape(144, D)
    xn[0:ROWS1] = normalize(x_ref[...].astype(F32))
    zsend(1)
    step_a(0)
    zsend(2)
    step_b(0)
    step_a(1)
    step_c(0)
    step_d(0)
    step_b(1)
    step_a(2)
    step_e(0)
    project_qkv(0, ROWS1)
    attend(0, 144, None)
    attend(144, 144, None)
    first[...] = (x_ref[...].astype(F32) + project_out(0, ROWS1)).astype(BF16)
    msg_out[...] = dot(p_send[...], first[...]).astype(BF16)
    halo_first = exchange(0, msg_out, msg_in, halo_down)
    stay = dot(p_own[...], first[...])
    step_c(1)
    step_b(2)
    step_d(1)
    for copy in halo_first:
        copy.wait_recv()
    second[...] = (stay + dot(p_arrive[...], msg_in[...])).astype(BF16)
    xn[...] = normalize(second[...].astype(F32))
    step_e(1)
    project_qkv(1, ROWS2)
    last = (lat == lats - 1).astype(F32)

    def attend_shifted(group):
        bias = bias_ref[0]
        if group >= 2:
            bias = bias + last * bias_ref[1]
        attend(group * GROUP, GROUP, jnp.concatenate([bias] * 4, axis=0))

    for group in range(2):
        attend_shifted(group)
    step_c(2)
    for group in range(2, 4):
        attend_shifted(group)
    second[...] = (second[...].astype(F32) + project_out(1, ROWS2)).astype(BF16)
    ret_out[...] = dot(p_back[...], second[...]).astype(BF16)
    halo_second = exchange(1, ret_out, ret_in, halo_up)
    stay = dot(p_qown[...], second[...])
    step_d(2)
    for copy in halo_second:
        copy.wait_recv()
    quads = stay + dot(p_qedge[...], ret_in[...])
    quads = jnp.concatenate([quads[GROUP * p : GROUP * (p + 1)] for p in range(4)], axis=1)
    quads = normalize(quads)
    step_e(2)
    merged = jnp.zeros((GROUP, 2 * D), F32)
    for p in range(4):
        w = G[2 + p // 2].reshape(2 * Z, 2, 32, D)[:, p % 2].reshape(2 * D, D)
        merged += dot_nt(quads[:, p * D : (p + 1) * D], w)
    out_ref[...] = merged[0:72].astype(BF16)

    for copy in halo_first + halo_second:
        copy.wait_send()
    for u in range(len(UNITS)):
        drain(zbytes(u), zs.at[u])
        for axis in range(2):
            drain(p1bytes(u), p1s.at[u, axis])
            for way in range(3 if DIRECT[u] else 2):
                drain(wide(u, axis, mine[axis], 0, H), p2s.at[u, axis, way])
            if not DIRECT[u]:
                for way in range(2):
                    drain(wide(u, axis, mine[axis], 0, Q), p3s.at[u, axis, way])
        drain(G.at[of(u), :, :, :, c], ss.at[u])


def call(tokens, *columns):
    vmem = pl.BlockSpec(memory_space=pltpu.VMEM)
    dma = pltpu.SemaphoreType.DMA
    return pl.pallas_call(
        kernel,
        out_shape=jax.ShapeDtypeStruct((72, 2 * D), BF16),
        in_specs=[pl.BlockSpec(memory_space=pl.ANY)] * 6,
        out_specs=vmem,
        scratch_shapes=[
            pltpu.VMEM((SLABS, Z, 2, 2, 2, 16, D), BF16),
            pltpu.VMEM((2, 64, D), F32),
            pltpu.VMEM((SLABS, 4, 16, L), BF16),
            pltpu.VMEM((12, ROWS2, 128), BF16),
            pltpu.VMEM((4, ROWS2, 128), BF16),
            pltpu.VMEM((ROWS1, D), BF16),
            pltpu.VMEM((ROWS2, D), BF16),
            pltpu.VMEM((ROWS2, D), BF16),
            pltpu.VMEM((MSG, D), BF16),
            pltpu.VMEM((MSG, D), BF16),
            pltpu.VMEM((MSG, D), BF16),
            pltpu.VMEM((MSG, D), BF16),
        ]
        + [pltpu.VMEM(p[:2], BF16) for p in PERMUTATIONS]
        + [
            pltpu.VMEM((2, GROUP, GROUP), F32),
            pltpu.VMEM((24, D), BF16),
            pltpu.VMEM((8, D), BF16),
            pltpu.VMEM((24, D), BF16),
            pltpu.VMEM((8, D), BF16),
            pltpu.VMEM((16, 4 * D), BF16),
            pltpu.VMEM((12, 12, 2, D), BF16),
            pltpu.VMEM((ROWS1, D), BF16),
            dma((6,)),
            dma((len(UNITS),)), dma(()), dma(()), dma((len(UNITS),)), dma((len(UNITS),)),
            dma((len(UNITS), 2)), dma((len(UNITS), 2)),
            dma((len(UNITS), 2, 3)), dma((len(UNITS), 2, 3)), dma((len(UNITS), 2, 2)), dma((len(UNITS), 2, 2)),
            dma((len(UNITS),)), dma((len(UNITS),)), dma((2, 3)), dma((2, 3)),
        ],
        compiler_params=pltpu.CompilerParams(
            collective_id=0, has_side_effects=True, vmem_limit_bytes=60 * 1024 * 1024
        ),
        name="swin",
    )(tokens, *columns)


def body(patches, qkv_first, proj_first, qkv_second, proj_second, merge_weight):
    merged = call(
        patches, qkv_first.T, proj_first.T, qkv_second.T, proj_second.T, merge_weight.T
    )
    return merged.reshape(6, 6, 2, 2 * D)


def solution(mesh):
    placed = (
        P("lon", "lat", None, None),
        P(None, "lon"),
        P(None, "lon"),
        P(None, "lon"),
        P(None, "lon"),
        P(None, "lon"),
    )
    return jax.shard_map(
        body, mesh=mesh, in_specs=placed, out_specs=P("lon", "lat", None, None), check_vma=False
    )
```

```python
import functools

import jax
import jax.numpy as jnp
from jax import lax
from jax.experimental import pallas as pl
from jax.experimental.pallas import tpu as pltpu
from jax.sharding import PartitionSpec as P

D = 512
HEADS = 16
Z = 16
H = Z // 2
Q = H // 2
L = D // 4
SLABS = 4
UNITS = ((0, 1), (1, 1), (2, 2))
DIRECT = (True, False, False)
WAYS = ((0, 1), (1, -1), (2, 2))
ROWS1 = 288
GROUP = 80
ROWS2 = 4 * GROUP
MSG = 208
EDGES = ((0, 112), (112, 48), (160, 48))
norm_epsilon = 1e-05
masked_score = -1e30
EXP2_SCALE = 32 ** (-0.5) * 1.4426950408889634
MESH = pl.DeviceIdType.MESH
F32 = jnp.float32
BF16 = jnp.bfloat16


def split(values, n):
    quotient = jnp.floor((values + 0.5) * (1.0 / n))
    return quotient, values - n * quotient


def both(*conditions):
    return functools.reduce(jnp.logical_and, conditions)


def edge_row(lo, la, lv):
    near = jnp.where(lo < 6, 160 + (lo * 3 + la) * 2 + lv, 112 + ((lo - 6) * 3 + la) * 2 + lv)
    return jnp.where(both(lo < 6, la >= 3), (lo * 9 + la - 3) * 2 + lv, near)


def first_row(lo, la, lv):
    window, rest = split(la, 6)
    return window * 144 + lo * 12 + rest * 2 + lv


def shifted_row(lo, la, lv):
    window, rest = split(jnp.where(la < 3, la + 9, la - 3), 6)
    return (window * 2 + lv) * GROUP + jnp.where(lo < 6, lo + 6, lo - 6) * 6 + rest


def edge_tokens(row):
    start = jnp.where(row < 112, 0, jnp.where(row < 160, 112, 160))
    half, lv = split(row - start, 2)
    lo9, la9 = split(half, 9)
    lo3, la3 = split(half, 3)
    wide = row < 112
    lo = jnp.where(wide, lo9, jnp.where(row < 160, lo3 + 6, lo3))
    la = jnp.where(wide, la9 + 3, la3)
    return lo, la, lv, half < jnp.where(wide, 54, 18)


def shifted_tokens(row):
    group, place = split(row, GROUP)
    window, lv = split(group, 2)
    slo, sla = split(place, 6)
    la = window * 6 + sla + 3
    lo = jnp.where(slo < 6, slo + 6, slo - 6)
    return lo, jnp.where(la < 12, la, la - 12), lv, place < 72


def quad_tokens(row):
    part, place = split(row, GROUP)
    odd_lat, odd_lon = split(part, 2)
    half, lv = split(place, 2)
    i, j = split(half, 6)
    return 2 * i + odd_lon, 2 * j + odd_lat, lv, place < 72


def one_hot(rows, columns, column_of):
    row = lax.broadcasted_iota(jnp.int32, (rows, 1), 0).astype(F32)
    at, valid = column_of(row)
    at = jnp.where(valid, at, -1.0)
    column = lax.broadcasted_iota(jnp.int32, (rows, columns), 1).astype(F32)
    return jnp.where(column == at, 1.0, 0.0).astype(BF16)


def column_send(row):
    lo, la, lv, valid = edge_tokens(row)
    return first_row(lo, la, lv), valid


def column_back(row):
    lo, la, lv, valid = edge_tokens(row)
    return shifted_row(lo, la, lv), valid


def kept(lo, la):
    return both(lo >= 6, la >= 3)


def column_own(row):
    lo, la, lv, valid = shifted_tokens(row)
    return first_row(lo, la, lv), both(valid, kept(lo, la))


def column_arrive(row):
    lo, la, lv, valid = shifted_tokens(row)
    return edge_row(lo, la, lv), both(valid, jnp.logical_not(kept(lo, la)))


def column_quad_own(row):
    lo, la, lv, valid = quad_tokens(row)
    return shifted_row(lo, la, lv), both(valid, kept(lo, la))


def column_quad_edge(row):
    lo, la, lv, valid = quad_tokens(row)
    return edge_row(lo, la, lv), both(valid, jnp.logical_not(kept(lo, la)))


PERMUTATIONS = (
    (MSG, ROWS1, column_send),
    (ROWS2, ROWS1, column_own),
    (ROWS2, MSG, column_arrive),
    (MSG, ROWS2, column_back),
    (4 * GROUP, ROWS2, column_quad_own),
    (4 * GROUP, MSG, column_quad_edge),
)


def normalize(values):
    centred = values - jnp.mean(values, axis=-1, keepdims=True)
    variance = jnp.mean(centred * centred, axis=-1, keepdims=True)
    return (centred * lax.rsqrt(variance + norm_epsilon)).astype(BF16)


def dot_nt(a, b):
    return lax.dot_general(a, b, (((1,), (1,)), ((), ())), preferred_element_type=F32)


def dot(a, b):
    return jnp.dot(a, b, preferred_element_type=F32)


def kernel(
    x_hbm, q1_hbm, o1_hbm, q2_hbm, o2_hbm, merge_hbm, out_ref,
    G, E, piece, qkv, mix, first, second, xn, msg_out, msg_in, ret_out, ret_in,
    p_send, p_own, p_arrive, p_back, p_qown, p_qedge, bias_ref, q1, o1, q2, o2, merge, grid, x_ref,
    wsem, lsem, es, er, zs, zr, p1s, p1r, p2s, p2r, p3s, p3r, ss, sr, hs, hr,
):
    lon, lat = lax.axis_index("lon"), lax.axis_index("lat")
    lons, lats = 4 * Z, 8
    c = lax.rem(lon, 2)
    yh = lax.rem(lon // 2, 2)
    z = lon // 4
    x = lax.rem(lat, 4)
    yl = lat // 4
    y = yh * 2 + yl
    lanes = pl.ds(pl.multiple_of(x * L, L), L)

    def place(x, y, z, c):
        return ((z * 2 + y // 2) * 2 + c, lax.rem(y, 2) * 4 + x)

    def wrap4(v):
        return lax.rem(v + 4, 4)

    sibling = place(x, y, z, 1 - c)
    lon_up, lon_down = lax.rem(lon + 1, lons), lax.rem(lon + lons - 1, lons)
    lat_up, lat_down = lax.rem(lat + 1, lats), lax.rem(lat + lats - 1, lats)
    halo_down = ((lon_down, lat), (lon, lat_down), (lon_down, lat_down))
    halo_up = ((lon_up, lat), (lon, lat_up), (lon_up, lat_up))

    def remote(src, dst, send, recv, device):
        return pltpu.make_async_remote_copy(
            src_ref=src, dst_ref=dst, send_sem=send, recv_sem=recv,
            device_id=device, device_id_type=MESH,
        )

    def drain(ref, sem):
        pltpu.make_async_copy(ref, ref, sem).wait()

    own_columns = ((q1_hbm, q1), (o1_hbm, o1), (q2_hbm, q2), (o2_hbm, o2), (merge_hbm, merge))
    grid_load = pltpu.make_async_copy(x_hbm, grid, wsem.at[5])
    grid_load.start()
    loads = [
        pltpu.make_async_copy(src, dst, wsem.at[i]) for i, (src, dst) in enumerate(own_columns)
    ]
    for load in loads:
        load.start()

    barrier = pltpu.get_barrier_semaphore()

    def greet(device):
        pl.semaphore_signal(barrier, inc=1, device_id=device, device_id_type=MESH)

    def distance(k):
        return 8 + (1 - 2 * lax.rem(k + 1, 2)) * ((k + 1) // 2)

    @pl.loop(0, Z - 1)
    def _(k):
        greet(place(x, y, lax.rem(z + distance(k), Z), c))

    for d in (2, 1, 3):
        greet(place(wrap4(x + d), y, z, c))
        greet(place(x, wrap4(y + d), z, c))
    for device in halo_down + halo_up:
        greet(device)
    greet(sibling)

    for load in loads:
        load.wait()
    for ref, start, n in ((q1, 0, 24), (o1, 24, 8), (q2, 32, 24), (o2, 56, 8)):
        E[c, start : start + n] = ref[...].astype(F32)
    pl.semaphore_wait(barrier, 1 + Z - 1 + 6 + 6)
    to_sibling = remote(E.at[c], E.at[c], es, er, sibling)
    to_sibling.start()

    low, high = (yl == 0).astype(F32), (yl == 1).astype(F32)
    core0, core1 = (c == 0).astype(F32), (c == 1).astype(F32)

    def put_piece(u, tile):
        tile = tile.astype(BF16)
        for k in range(4):
            piece[u, k] = tile[:, k * L : (k + 1) * L]

    for m in range(2):
        rows = merge[:, 2 * m * D : 2 * (m + 1) * D].astype(F32)
        put_piece(2 + m, rows[:, 0:D] * low + rows[:, D : 2 * D] * high)
    to_sibling.wait()
    for s in range(2):
        r0, r1 = E[0, 32 * s : 32 * s + 32], E[1, 32 * s : 32 * s + 32]
        tile = (low * core0) * r0[0:16]
        tile += (low * core1) * jnp.concatenate([r0[16:24], r1[0:8]], axis=0)
        tile += (high * core0) * r1[8:24]
        tile += (high * core1) * jnp.concatenate([r0[24:32], r1[24:32]], axis=0)
        put_piece(s, tile)

    def of(u):
        return pl.ds(*UNITS[u])

    def home(u):
        return G.at[of(u), z, yh, yl, c, :, lanes]

    def zsend(u):
        src, slot = piece.at[of(u), x], home(u)
        pltpu.make_async_copy(src, slot, lsem.at[u]).start()

        @pl.loop(0, Z - 1)
        def _(k):
            device = place(x, y, lax.rem(z + distance(k), Z), c)
            remote(src, slot, zs.at[u], zr.at[u], device).start()

    def zbytes(u):
        return G.at[of(u), 0 : Z - 1, yh, yl, c, :, lanes]

    def p1bytes(u):
        return G.at[of(u), 0:H, 0, 0, 0, :, 0 : 3 * L]

    def step_a(u):
        pltpu.make_async_copy(piece.at[of(u), x], home(u), lsem.at[u]).wait()
        drain(zbytes(u), zr.at[u])
        half0 = G.at[of(u), 0:H, yh, yl, c, :, lanes]
        half1 = G.at[of(u), H:Z, yh, yl, c, :, lanes]
        for d in (2, 1, 3):
            remote(half0, half0, p1s.at[u, 0], p1r.at[u, 0], place(wrap4(x + d), y, z, c)).start()
            remote(half1, half1, p1s.at[u, 1], p1r.at[u, 1], place(x, wrap4(y + d), z, c)).start()

    def wide(u, axis, at, z0, n):
        if axis == 0:
            return G.at[of(u), pl.ds(z0, n), at // 2, lax.rem(at, 2), c]
        span = pl.ds(pl.multiple_of(at * L, L), L)
        return G.at[of(u), pl.ds(H + z0, n), :, :, c, :, span]

    def along(axis, at):
        return place(x, at, z, c) if axis == 0 else place(at, y, z, c)

    mine = (y, x)

    def to_core(u, axis, at):
        ref = wide(u, axis, at, 0, H)
        remote(ref, ref, ss.at[u], sr.at[u], sibling).start()

    def step_b(u):
        for axis in range(2):
            drain(p1bytes(u), p1r.at[u, axis])
            ref = wide(u, axis, mine[axis], 0, H)
            for way, step in WAYS[: 3 if DIRECT[u] else 2]:
                remote(
                    ref, ref, p2s.at[u, axis, way], p2r.at[u, axis, way],
                    along(axis, wrap4(mine[axis] + step)),
                ).start()
        for axis in range(2):
            to_core(u, axis, mine[axis])

    def step_c(u):
        for axis in range(2):
            for way, step in WAYS[:2]:
                drain(wide(u, axis, mine[axis], 0, H), p2r.at[u, axis, way])
                if not DIRECT[u]:
                    ref = wide(u, axis, wrap4(mine[axis] - step), way * Q, Q)
                    remote(
                        ref, ref, p3s.at[u, axis, way], p3r.at[u, axis, way],
                        along(axis, wrap4(mine[axis] + step)),
                    ).start()
        for axis in range(2):
            for way, step in WAYS[:2]:
                to_core(u, axis, wrap4(mine[axis] + step))

    def step_d(u):
        for axis in range(2):
            if DIRECT[u]:
                drain(wide(u, axis, mine[axis], 0, H), p2r.at[u, axis, 2])
            else:
                for way in range(2):
                    drain(wide(u, axis, mine[axis], 0, Q), p3r.at[u, axis, way])
            to_core(u, axis, wrap4(mine[axis] + 2))

    def step_e(u):
        drain(G.at[of(u), :, :, :, c], sr.at[u])

    lane = lax.broadcasted_iota(jnp.int32, (1, 128), 1) // 32
    head_f32 = [(lane == h).astype(F32) for h in range(4)]
    head_bf16 = [mask.astype(BF16) for mask in head_f32]

    def project_qkv(u, rows):
        w = G[u].reshape(2 * Z, 4, 16, D)[:, 0:3].reshape(3 * D, D)
        for i in range(3):
            r = dot_nt(xn[0:rows], w[D * i : D * (i + 1)]).astype(BF16)
            for j in range(4):
                qkv[i * 4 + j, 0:rows] = r[:, 128 * j : 128 * j + 128]

    def attend(start, n, bias):
        rows = pl.ds(start, n)
        for g in range(4):
            q, k, v = qkv[g, rows], qkv[4 + g, rows], qkv[8 + g, rows]
            stacked = jnp.concatenate([q * mask for mask in head_bf16], axis=0)
            scores = dot_nt(stacked, k)
            if bias is not None:
                scores = scores + bias
            highest = jnp.max(scores, axis=-1, keepdims=True)
            weights = jnp.exp2((scores - highest) * EXP2_SCALE).astype(BF16)
            summed = dot(weights, jnp.concatenate([v, jnp.ones_like(v)], axis=1))
            total = head_f32[0] * summed[0:n, 0:128]
            norm = head_f32[0] * summed[0:n, 128:256]
            for h in range(1, 4):
                total += head_f32[h] * summed[h * n : (h + 1) * n, 0:128]
                norm += head_f32[h] * summed[h * n : (h + 1) * n, 128:256]
            mix[g, rows] = (total / norm).astype(BF16)

    def project_out(u, rows):
        w = G[u].reshape(2 * Z, 4, 16, D)[:, 3].reshape(D, D)
        mixed = jnp.concatenate([mix[g, 0:rows] for g in range(4)], axis=1)
        return dot_nt(mixed, w)

    def exchange(k, src, dst, devices):
        copies = []
        for i in (2, 1, 0):
            start, n = EDGES[i]
            ref, to = src.at[pl.ds(start, n)], dst.at[pl.ds(start, n)]
            copies.append(remote(ref, to, hs.at[k, i], hr.at[k, i], devices[i]))
            copies[-1].start()
        return copies

    zsend(0)
    for ref, (rows, columns, column_of) in zip(
        (p_send, p_own, p_arrive, p_back, p_qown, p_qedge), PERMUTATIONS
    ):
        ref[...] = one_hot(rows, columns, column_of)
    row = lax.broadcasted_iota(jnp.int32, (GROUP, GROUP), 0).astype(F32)
    column = lax.broadcasted_iota(jnp.int32, (GROUP, GROUP), 1).astype(F32)
    bias_ref[0] = jnp.where(column < 72, 0.0, masked_score)
    north = split(row, 6)[1] < 3
    bias_ref[1] = jnp.where(north == (split(column, 6)[1] < 3), 0.0, masked_score)
    grid_load.wait()
    for w in range(2):
        x_ref[144 * w : 144 * w + 144] = grid[:, 6 * w : 6 * w + 6].reshape(144, D)
    xn[0:ROWS1] = normalize(x_ref[...].astype(F32))
    zsend(1)
    step_a(0)
    zsend(2)
    step_b(0)
    step_a(1)
    step_c(0)
    step_d(0)
    step_b(1)
    step_a(2)
    step_e(0)
    project_qkv(0, ROWS1)
    attend(0, 144, None)
    attend(144, 144, None)
    first[...] = (x_ref[...].astype(F32) + project_out(0, ROWS1)).astype(BF16)
    msg_out[...] = dot(p_send[...], first[...]).astype(BF16)
    halo_first = exchange(0, msg_out, msg_in, halo_down)
    stay = dot(p_own[...], first[...])
    step_c(1)
    step_b(2)
    step_d(1)
    for copy in halo_first:
        copy.wait_recv()
    second[...] = (stay + dot(p_arrive[...], msg_in[...])).astype(BF16)
    xn[...] = normalize(second[...].astype(F32))
    step_e(1)
    project_qkv(1, ROWS2)
    last = (lat == lats - 1).astype(F32)

    def attend_shifted(group):
        bias = bias_ref[0]
        if group >= 2:
            bias = bias + last * bias_ref[1]
        attend(group * GROUP, GROUP, jnp.concatenate([bias] * 4, axis=0))

    for group in range(2):
        attend_shifted(group)
    step_c(2)
    for group in range(2, 4):
        attend_shifted(group)
    second[...] = (second[...].astype(F32) + project_out(1, ROWS2)).astype(BF16)
    ret_out[...] = dot(p_back[...], second[...]).astype(BF16)
    halo_second = exchange(1, ret_out, ret_in, halo_up)
    stay = dot(p_qown[...], second[...])
    step_d(2)
    for copy in halo_second:
        copy.wait_recv()
    quads = stay + dot(p_qedge[...], ret_in[...])
    quads = jnp.concatenate([quads[GROUP * p : GROUP * (p + 1)] for p in range(4)], axis=1)
    quads = normalize(quads)
    step_e(2)
    merged = jnp.zeros((GROUP, 2 * D), F32)
    for p in range(4):
        w = G[2 + p // 2].reshape(2 * Z, 2, 32, D)[:, p % 2].reshape(2 * D, D)
        merged += dot_nt(quads[:, p * D : (p + 1) * D], w)
    out_ref[...] = merged[0:72].astype(BF16)

    for copy in halo_first + halo_second:
        copy.wait_send()
    for u in range(len(UNITS)):
        drain(zbytes(u), zs.at[u])
        for axis in range(2):
            drain(p1bytes(u), p1s.at[u, axis])
            for way in range(3 if DIRECT[u] else 2):
                drain(wide(u, axis, mine[axis], 0, H), p2s.at[u, axis, way])
            if not DIRECT[u]:
                for way in range(2):
                    drain(wide(u, axis, mine[axis], 0, Q), p3s.at[u, axis, way])
        drain(G.at[of(u), :, :, :, c], ss.at[u])


def call(tokens, *columns):
    vmem = pl.BlockSpec(memory_space=pltpu.VMEM)
    dma = pltpu.SemaphoreType.DMA
    return pl.pallas_call(
        kernel,
        out_shape=jax.ShapeDtypeStruct((72, 2 * D), BF16),
        in_specs=[pl.BlockSpec(memory_space=pl.ANY)] * 6,
        out_specs=vmem,
        scratch_shapes=[
            pltpu.VMEM((SLABS, Z, 2, 2, 2, 16, D), BF16),
            pltpu.VMEM((2, 64, D), F32),
            pltpu.VMEM((SLABS, 4, 16, L), BF16),
            pltpu.VMEM((12, ROWS2, 128), BF16),
            pltpu.VMEM((4, ROWS2, 128), BF16),
            pltpu.VMEM((ROWS1, D), BF16),
            pltpu.VMEM((ROWS2, D), BF16),
            pltpu.VMEM((ROWS2, D), BF16),
            pltpu.VMEM((MSG, D), BF16),
            pltpu.VMEM((MSG, D), BF16),
            pltpu.VMEM((MSG, D), BF16),
            pltpu.VMEM((MSG, D), BF16),
        ]
        + [pltpu.VMEM(p[:2], BF16) for p in PERMUTATIONS]
        + [
            pltpu.VMEM((2, GROUP, GROUP), F32),
            pltpu.VMEM((24, D), BF16),
            pltpu.VMEM((8, D), BF16),
            pltpu.VMEM((24, D), BF16),
            pltpu.VMEM((8, D), BF16),
            pltpu.VMEM((16, 4 * D), BF16),
            pltpu.VMEM((12, 12, 2, D), BF16),
            pltpu.VMEM((ROWS1, D), BF16),
            dma((6,)),
            dma((len(UNITS),)), dma(()), dma(()), dma((len(UNITS),)), dma((len(UNITS),)),
            dma((len(UNITS), 2)), dma((len(UNITS), 2)),
            dma((len(UNITS), 2, 3)), dma((len(UNITS), 2, 3)), dma((len(UNITS), 2, 2)), dma((len(UNITS), 2, 2)),
            dma((len(UNITS),)), dma((len(UNITS),)), dma((2, 3)), dma((2, 3)),
        ],
        compiler_params=pltpu.CompilerParams(
            collective_id=0, has_side_effects=True, vmem_limit_bytes=60 * 1024 * 1024
        ),
        name="swin",
    )(tokens, *columns)


def body(patches, qkv_first, proj_first, qkv_second, proj_second, merge_weight):
    merged = call(
        patches, qkv_first.T, proj_first.T, qkv_second.T, proj_second.T, merge_weight.T
    )
    return merged.reshape(6, 6, 2, 2 * D)


def solution(mesh):
    placed = (
        P("lon", "lat", None, None),
        P(None, "lon"),
        P(None, "lon"),
        P(None, "lon"),
        P(None, "lon"),
        P(None, "lon"),
    )
    return jax.shard_map(
        body, mesh=mesh, in_specs=placed, out_specs=P("lon", "lat", None, None), check_vma=False
    )
```

```python
import functools

import jax
import jax.numpy as jnp
from jax import lax
from jax.experimental import pallas as pl
from jax.experimental.pallas import tpu as pltpu
from jax.sharding import PartitionSpec as P

D = 512
HEADS = 16
Z = 16
H = Z // 2
Q = H // 2
L = D // 4
SLABS = 4
UNITS = ((0, 1), (1, 1), (2, 2))
DIRECT = (True, False, False)
WAYS = ((0, 1), (1, -1), (2, 2))
ROWS1 = 288
GROUP = 80
ROWS2 = 4 * GROUP
MSG = 208
EDGES = ((0, 112), (112, 48), (160, 48))
norm_epsilon = 1e-05
masked_score = -1e30
EXP2_SCALE = 32 ** (-0.5) * 1.4426950408889634
MESH = pl.DeviceIdType.MESH
F32 = jnp.float32
BF16 = jnp.bfloat16


def split(values, n):
    quotient = jnp.floor((values + 0.5) * (1.0 / n))
    return quotient, values - n * quotient


def both(*conditions):
    return functools.reduce(jnp.logical_and, conditions)


def edge_row(lo, la, lv):
    near = jnp.where(lo < 6, 160 + (lo * 3 + la) * 2 + lv, 112 + ((lo - 6) * 3 + la) * 2 + lv)
    return jnp.where(both(lo < 6, la >= 3), (lo * 9 + la - 3) * 2 + lv, near)


def first_row(lo, la, lv):
    window, rest = split(la, 6)
    return window * 144 + lo * 12 + rest * 2 + lv


def shifted_row(lo, la, lv):
    window, rest = split(jnp.where(la < 3, la + 9, la - 3), 6)
    return (window * 2 + lv) * GROUP + jnp.where(lo < 6, lo + 6, lo - 6) * 6 + rest


def edge_tokens(row):
    start = jnp.where(row < 112, 0, jnp.where(row < 160, 112, 160))
    half, lv = split(row - start, 2)
    lo9, la9 = split(half, 9)
    lo3, la3 = split(half, 3)
    wide = row < 112
    lo = jnp.where(wide, lo9, jnp.where(row < 160, lo3 + 6, lo3))
    la = jnp.where(wide, la9 + 3, la3)
    return lo, la, lv, half < jnp.where(wide, 54, 18)


def shifted_tokens(row):
    group, place = split(row, GROUP)
    window, lv = split(group, 2)
    slo, sla = split(place, 6)
    la = window * 6 + sla + 3
    lo = jnp.where(slo < 6, slo + 6, slo - 6)
    return lo, jnp.where(la < 12, la, la - 12), lv, place < 72


def quad_tokens(row):
    part, place = split(row, GROUP)
    odd_lat, odd_lon = split(part, 2)
    half, lv = split(place, 2)
    i, j = split(half, 6)
    return 2 * i + odd_lon, 2 * j + odd_lat, lv, place < 72


def one_hot(rows, columns, column_of):
    row = lax.broadcasted_iota(jnp.int32, (rows, 1), 0).astype(F32)
    at, valid = column_of(row)
    at = jnp.where(valid, at, -1.0)
    column = lax.broadcasted_iota(jnp.int32, (rows, columns), 1).astype(F32)
    return jnp.where(column == at, 1.0, 0.0).astype(BF16)


def column_send(row):
    lo, la, lv, valid = edge_tokens(row)
    return first_row(lo, la, lv), valid


def column_back(row):
    lo, la, lv, valid = edge_tokens(row)
    return shifted_row(lo, la, lv), valid


def kept(lo, la):
    return both(lo >= 6, la >= 3)


def column_own(row):
    lo, la, lv, valid = shifted_tokens(row)
    return first_row(lo, la, lv), both(valid, kept(lo, la))


def column_arrive(row):
    lo, la, lv, valid = shifted_tokens(row)
    return edge_row(lo, la, lv), both(valid, jnp.logical_not(kept(lo, la)))


def column_quad_own(row):
    lo, la, lv, valid = quad_tokens(row)
    return shifted_row(lo, la, lv), both(valid, kept(lo, la))


def column_quad_edge(row):
    lo, la, lv, valid = quad_tokens(row)
    return edge_row(lo, la, lv), both(valid, jnp.logical_not(kept(lo, la)))


PERMUTATIONS = (
    (MSG, ROWS1, column_send),
    (ROWS2, ROWS1, column_own),
    (ROWS2, MSG, column_arrive),
    (MSG, ROWS2, column_back),
    (4 * GROUP, ROWS2, column_quad_own),
    (4 * GROUP, MSG, column_quad_edge),
)


def normalize(values):
    centred = values - jnp.mean(values, axis=-1, keepdims=True)
    variance = jnp.mean(centred * centred, axis=-1, keepdims=True)
    return (centred * lax.rsqrt(variance + norm_epsilon)).astype(BF16)


def dot_nt(a, b):
    return lax.dot_general(a, b, (((1,), (1,)), ((), ())), preferred_element_type=F32)


def dot(a, b):
    return jnp.dot(a, b, preferred_element_type=F32)


def kernel(
    x_hbm, q1_hbm, o1_hbm, q2_hbm, o2_hbm, merge_hbm, out_ref,
    G, E, piece, qkv, mix, first, second, xn, msg_out, msg_in, ret_out, ret_in,
    p_send, p_own, p_arrive, p_back, p_qown, p_qedge, bias_ref, q1, o1, q2, o2, merge, grid, x_ref,
    wsem, lsem, es, er, zs, zr, p1s, p1r, p2s, p2r, p3s, p3r, ss, sr, hs, hr,
):
    lon, lat = lax.axis_index("lon"), lax.axis_index("lat")
    lons, lats = 4 * Z, 8
    c = lax.rem(lon, 2)
    yh = lax.rem(lon // 2, 2)
    z = lon // 4
    x = lax.rem(lat, 4)
    yl = lat // 4
    y = yh * 2 + yl
    lanes = pl.ds(pl.multiple_of(x * L, L), L)

    def place(x, y, z, c):
        return ((z * 2 + y // 2) * 2 + c, lax.rem(y, 2) * 4 + x)

    def wrap4(v):
        return lax.rem(v + 4, 4)

    sibling = place(x, y, z, 1 - c)
    lon_up, lon_down = lax.rem(lon + 1, lons), lax.rem(lon + lons - 1, lons)
    lat_up, lat_down = lax.rem(lat + 1, lats), lax.rem(lat + lats - 1, lats)
    halo_down = ((lon_down, lat), (lon, lat_down), (lon_down, lat_down))
    halo_up = ((lon_up, lat), (lon, lat_up), (lon_up, lat_up))

    def remote(src, dst, send, recv, device):
        return pltpu.make_async_remote_copy(
            src_ref=src, dst_ref=dst, send_sem=send, recv_sem=recv,
            device_id=device, device_id_type=MESH,
        )

    def drain(ref, sem):
        pltpu.make_async_copy(ref, ref, sem).wait()

    own_columns = ((q1_hbm, q1), (o1_hbm, o1), (q2_hbm, q2), (o2_hbm, o2), (merge_hbm, merge))
    grid_load = pltpu.make_async_copy(x_hbm, grid, wsem.at[5])
    grid_load.start()
    loads = [
        pltpu.make_async_copy(src, dst, wsem.at[i]) for i, (src, dst) in enumerate(own_columns)
    ]
    for load in loads:
        load.start()

    barrier = pltpu.get_barrier_semaphore()

    def greet(device):
        pl.semaphore_signal(barrier, inc=1, device_id=device, device_id_type=MESH)

    def distance(k):
        return 8 + (1 - 2 * lax.rem(k + 1, 2)) * ((k + 1) // 2)

    @pl.loop(0, Z - 1)
    def _(k):
        greet(place(x, y, lax.rem(z + distance(k), Z), c))

    for d in (2, 1, 3):
        greet(place(wrap4(x + d), y, z, c))
        greet(place(x, wrap4(y + d), z, c))
    for device in halo_down + halo_up:
        greet(device)
    greet(sibling)

    for load in loads:
        load.wait()
    for ref, start, n in ((q1, 0, 24), (o1, 24, 8), (q2, 32, 24), (o2, 56, 8)):
        E[c, start : start + n] = ref[...].astype(F32)
    pl.semaphore_wait(barrier, 1 + Z - 1 + 6 + 6)
    to_sibling = remote(E.at[c], E.at[c], es, er, sibling)
    to_sibling.start()

    low, high = (yl == 0).astype(F32), (yl == 1).astype(F32)
    core0, core1 = (c == 0).astype(F32), (c == 1).astype(F32)

    def put_piece(u, tile):
        tile = tile.astype(BF16)
        for k in range(4):
            piece[u, k] = tile[:, k * L : (k + 1) * L]

    for m in range(2):
        rows = merge[:, 2 * m * D : 2 * (m + 1) * D].astype(F32)
        put_piece(2 + m, rows[:, 0:D] * low + rows[:, D : 2 * D] * high)
    to_sibling.wait()
    for s in range(2):
        r0, r1 = E[0, 32 * s : 32 * s + 32], E[1, 32 * s : 32 * s + 32]
        tile = (low * core0) * r0[0:16]
        tile += (low * core1) * jnp.concatenate([r0[16:24], r1[0:8]], axis=0)
        tile += (high * core0) * r1[8:24]
        tile += (high * core1) * jnp.concatenate([r0[24:32], r1[24:32]], axis=0)
        put_piece(s, tile)

    def of(u):
        return pl.ds(*UNITS[u])

    def home(u):
        return G.at[of(u), z, yh, yl, c, :, lanes]

    def zsend(u):
        src, slot = piece.at[of(u), x], home(u)
        pltpu.make_async_copy(src, slot, lsem.at[u]).start()

        @pl.loop(0, Z - 1)
        def _(k):
            device = place(x, y, lax.rem(z + distance(k), Z), c)
            remote(src, slot, zs.at[u], zr.at[u], device).start()

    def zbytes(u):
        return G.at[of(u), 0 : Z - 1, yh, yl, c, :, lanes]

    def p1bytes(u):
        return G.at[of(u), 0:H, 0, 0, 0, :, 0 : 3 * L]

    def step_a(u):
        pltpu.make_async_copy(piece.at[of(u), x], home(u), lsem.at[u]).wait()
        drain(zbytes(u), zr.at[u])
        half0 = G.at[of(u), 0:H, yh, yl, c, :, lanes]
        half1 = G.at[of(u), H:Z, yh, yl, c, :, lanes]
        for d in (2, 1, 3):
            remote(half0, half0, p1s.at[u, 0], p1r.at[u, 0], place(wrap4(x + d), y, z, c)).start()
            remote(half1, half1, p1s.at[u, 1], p1r.at[u, 1], place(x, wrap4(y + d), z, c)).start()

    def wide(u, axis, at, z0, n):
        if axis == 0:
            return G.at[of(u), pl.ds(z0, n), at // 2, lax.rem(at, 2), c]
        span = pl.ds(pl.multiple_of(at * L, L), L)
        return G.at[of(u), pl.ds(H + z0, n), :, :, c, :, span]

    def along(axis, at):
        return place(x, at, z, c) if axis == 0 else place(at, y, z, c)

    mine = (y, x)

    def to_core(u, axis, at):
        ref = wide(u, axis, at, 0, H)
        remote(ref, ref, ss.at[u], sr.at[u], sibling).start()

    def step_b(u):
        for axis in range(2):
            drain(p1bytes(u), p1r.at[u, axis])
            ref = wide(u, axis, mine[axis], 0, H)
            for way, step in WAYS[: 3 if DIRECT[u] else 2]:
                remote(
                    ref, ref, p2s.at[u, axis, way], p2r.at[u, axis, way],
                    along(axis, wrap4(mine[axis] + step)),
                ).start()
        for axis in range(2):
            to_core(u, axis, mine[axis])

    def step_c(u):
        for axis in range(2):
            for way, step in WAYS[:2]:
                drain(wide(u, axis, mine[axis], 0, H), p2r.at[u, axis, way])
                if not DIRECT[u]:
                    ref = wide(u, axis, wrap4(mine[axis] - step), way * Q, Q)
                    remote(
                        ref, ref, p3s.at[u, axis, way], p3r.at[u, axis, way],
                        along(axis, wrap4(mine[axis] + step)),
                    ).start()
        for axis in range(2):
            for way, step in WAYS[:2]:
                to_core(u, axis, wrap4(mine[axis] + step))

    def step_d(u):
        for axis in range(2):
            if DIRECT[u]:
                drain(wide(u, axis, mine[axis], 0, H), p2r.at[u, axis, 2])
            else:
                for way in range(2):
                    drain(wide(u, axis, mine[axis], 0, Q), p3r.at[u, axis, way])
            to_core(u, axis, wrap4(mine[axis] + 2))

    def step_e(u):
        drain(G.at[of(u), :, :, :, c], sr.at[u])

    lane = lax.broadcasted_iota(jnp.int32, (1, 128), 1) // 32
    head_f32 = [(lane == h).astype(F32) for h in range(4)]
    head_bf16 = [mask.astype(BF16) for mask in head_f32]

    def project_qkv(u, rows):
        w = G[u].reshape(2 * Z, 4, 16, D)[:, 0:3].reshape(3 * D, D)
        for i in range(3):
            r = dot_nt(xn[0:rows], w[D * i : D * (i + 1)]).astype(BF16)
            for j in range(4):
                qkv[i * 4 + j, 0:rows] = r[:, 128 * j : 128 * j + 128]

    def attend(start, n, bias):
        rows = pl.ds(start, n)
        for g in range(4):
            q, k, v = qkv[g, rows], qkv[4 + g, rows], qkv[8 + g, rows]
            stacked = jnp.concatenate([q * mask for mask in head_bf16], axis=0)
            scores = dot_nt(stacked, k)
            if bias is not None:
                scores = scores + bias
            highest = jnp.max(scores, axis=-1, keepdims=True)
            weights = jnp.exp2((scores - highest) * EXP2_SCALE).astype(BF16)
            summed = dot(weights, jnp.concatenate([v, jnp.ones_like(v)], axis=1))
            total = head_f32[0] * summed[0:n, 0:128]
            norm = head_f32[0] * summed[0:n, 128:256]
            for h in range(1, 4):
                total += head_f32[h] * summed[h * n : (h + 1) * n, 0:128]
                norm += head_f32[h] * summed[h * n : (h + 1) * n, 128:256]
            mix[g, rows] = (total / norm).astype(BF16)

    def project_out(u, rows):
        w = G[u].reshape(2 * Z, 4, 16, D)[:, 3].reshape(D, D)
        mixed = jnp.concatenate([mix[g, 0:rows] for g in range(4)], axis=1)
        return dot_nt(mixed, w)

    def exchange(k, src, dst, devices):
        copies = []
        for i in (2, 1, 0):
            start, n = EDGES[i]
            ref, to = src.at[pl.ds(start, n)], dst.at[pl.ds(start, n)]
            copies.append(remote(ref, to, hs.at[k, i], hr.at[k, i], devices[i]))
            copies[-1].start()
        return copies

    zsend(0)
    grid_load.wait()
    for w in range(2):
        x_ref[144 * w : 144 * w + 144] = grid[:, 6 * w : 6 * w + 6].reshape(144, D)
    xn[0:ROWS1] = normalize(x_ref[...].astype(F32))
    zsend(1)
    for ref, (rows, columns, column_of) in zip(
        (p_send, p_own, p_arrive, p_back, p_qown, p_qedge), PERMUTATIONS
    ):
        ref[...] = one_hot(rows, columns, column_of)
    row = lax.broadcasted_iota(jnp.int32, (GROUP, GROUP), 0).astype(F32)
    column = lax.broadcasted_iota(jnp.int32, (GROUP, GROUP), 1).astype(F32)
    bias_ref[0] = jnp.where(column < 72, 0.0, masked_score)
    north = split(row, 6)[1] < 3
    bias_ref[1] = jnp.where(north == (split(column, 6)[1] < 3), 0.0, masked_score)
    step_a(0)
    zsend(2)
    step_b(0)
    step_a(1)
    step_c(0)
    step_d(0)
    step_b(1)
    step_a(2)
    step_e(0)
    project_qkv(0, ROWS1)
    attend(0, 144, None)
    attend(144, 144, None)
    first[...] = (x_ref[...].astype(F32) + project_out(0, ROWS1)).astype(BF16)
    msg_out[...] = dot(p_send[...], first[...]).astype(BF16)
    halo_first = exchange(0, msg_out, msg_in, halo_down)
    stay = dot(p_own[...], first[...])
    step_c(1)
    step_b(2)
    step_d(1)
    for copy in halo_first:
        copy.wait_recv()
    second[...] = (stay + dot(p_arrive[...], msg_in[...])).astype(BF16)
    xn[...] = normalize(second[...].astype(F32))
    step_e(1)
    project_qkv(1, ROWS2)
    last = (lat == lats - 1).astype(F32)

    def attend_shifted(group):
        bias = bias_ref[0]
        if group >= 2:
            bias = bias + last * bias_ref[1]
        attend(group * GROUP, GROUP, jnp.concatenate([bias] * 4, axis=0))

    for group in range(2):
        attend_shifted(group)
    step_c(2)
    for group in range(2, 4):
        attend_shifted(group)
    second[...] = (second[...].astype(F32) + project_out(1, ROWS2)).astype(BF16)
    ret_out[...] = dot(p_back[...], second[...]).astype(BF16)
    halo_second = exchange(1, ret_out, ret_in, halo_up)
    stay = dot(p_qown[...], second[...])
    step_d(2)
    for copy in halo_second:
        copy.wait_recv()
    quads = stay + dot(p_qedge[...], ret_in[...])
    quads = jnp.concatenate([quads[GROUP * p : GROUP * (p + 1)] for p in range(4)], axis=1)
    quads = normalize(quads)
    step_e(2)
    merged = jnp.zeros((GROUP, 2 * D), F32)
    for p in range(4):
        w = G[2 + p // 2].reshape(2 * Z, 2, 32, D)[:, p % 2].reshape(2 * D, D)
        merged += dot_nt(quads[:, p * D : (p + 1) * D], w)
    out_ref[...] = merged[0:72].astype(BF16)

    for copy in halo_first + halo_second:
        copy.wait_send()
    for u in range(len(UNITS)):
        drain(zbytes(u), zs.at[u])
        for axis in range(2):
            drain(p1bytes(u), p1s.at[u, axis])
            for way in range(3 if DIRECT[u] else 2):
                drain(wide(u, axis, mine[axis], 0, H), p2s.at[u, axis, way])
            if not DIRECT[u]:
                for way in range(2):
                    drain(wide(u, axis, mine[axis], 0, Q), p3s.at[u, axis, way])
        drain(G.at[of(u), :, :, :, c], ss.at[u])


def call(tokens, *columns):
    vmem = pl.BlockSpec(memory_space=pltpu.VMEM)
    dma = pltpu.SemaphoreType.DMA
    return pl.pallas_call(
        kernel,
        out_shape=jax.ShapeDtypeStruct((72, 2 * D), BF16),
        in_specs=[pl.BlockSpec(memory_space=pl.ANY)] * 6,
        out_specs=vmem,
        scratch_shapes=[
            pltpu.VMEM((SLABS, Z, 2, 2, 2, 16, D), BF16),
            pltpu.VMEM((2, 64, D), F32),
            pltpu.VMEM((SLABS, 4, 16, L), BF16),
            pltpu.VMEM((12, ROWS2, 128), BF16),
            pltpu.VMEM((4, ROWS2, 128), BF16),
            pltpu.VMEM((ROWS1, D), BF16),
            pltpu.VMEM((ROWS2, D), BF16),
            pltpu.VMEM((ROWS2, D), BF16),
            pltpu.VMEM((MSG, D), BF16),
            pltpu.VMEM((MSG, D), BF16),
            pltpu.VMEM((MSG, D), BF16),
            pltpu.VMEM((MSG, D), BF16),
        ]
        + [pltpu.VMEM(p[:2], BF16) for p in PERMUTATIONS]
        + [
            pltpu.VMEM((2, GROUP, GROUP), F32),
            pltpu.VMEM((24, D), BF16),
            pltpu.VMEM((8, D), BF16),
            pltpu.VMEM((24, D), BF16),
            pltpu.VMEM((8, D), BF16),
            pltpu.VMEM((16, 4 * D), BF16),
            pltpu.VMEM((12, 12, 2, D), BF16),
            pltpu.VMEM((ROWS1, D), BF16),
            dma((6,)),
            dma((len(UNITS),)), dma(()), dma(()), dma((len(UNITS),)), dma((len(UNITS),)),
            dma((len(UNITS), 2)), dma((len(UNITS), 2)),
            dma((len(UNITS), 2, 3)), dma((len(UNITS), 2, 3)), dma((len(UNITS), 2, 2)), dma((len(UNITS), 2, 2)),
            dma((len(UNITS),)), dma((len(UNITS),)), dma((2, 3)), dma((2, 3)),
        ],
        compiler_params=pltpu.CompilerParams(
            collective_id=0, has_side_effects=True, vmem_limit_bytes=60 * 1024 * 1024
        ),
        name="swin",
    )(tokens, *columns)


def body(patches, qkv_first, proj_first, qkv_second, proj_second, merge_weight):
    merged = call(
        patches, qkv_first.T, proj_first.T, qkv_second.T, proj_second.T, merge_weight.T
    )
    return merged.reshape(6, 6, 2, 2 * D)


def solution(mesh):
    placed = (
        P("lon", "lat", None, None),
        P(None, "lon"),
        P(None, "lon"),
        P(None, "lon"),
        P(None, "lon"),
        P(None, "lon"),
    )
    return jax.shard_map(
        body, mesh=mesh, in_specs=placed, out_specs=P("lon", "lat", None, None), check_vma=False
    )
```
